256 devices in a mesh: group: 4 (over x), img: 32 (over z, y), tensor: 2 (over core).
Axes of the slice: x: 4, y: 4, z: 8, core: 2. Of those that a mesh axis runs over, the one named last changes fastest.
Arguments:
- features: bfloat16 [8, 4096, 8192], P('group', ('img', 'tensor')), may hold values from -6 to 6
- kv_weights: bfloat16 [2, 8192, 1024], P(None, 'img', 'tensor'), may hold values from -0.0625 to 0.0625
- key_gain: float32 [128], replicated, may hold values from 0.1 to 1.9
- queries: bfloat16 [1536, 8192], P('group', 'tensor'), may hold values from -70 to 70
- out_weight: bfloat16 [8192, 8192], P('tensor', 'img'), may hold values from -6 to 6
- attn_gate: float32 [1], replicated, may hold values from 0.4 to 1.5
- group_images: int32 [4, 2], replicated, may hold values from 0 to 7, as said below
- tile_valid: int32 [8, 4], replicated, may hold values from 1 to 1024
Outputs:
- gated: bfloat16 [1536, 8192], P(('group', 'tensor'), 'img')
The draws below stay inside these ranges and needn't reach their ends.
Inputs may be any that keep to these rules, and one draw needn't show every extreme that they name: `group_images`: every image appears exactly once. Image e is encoded at encoder index e // 2, and one group's images come from different encoder indices.
All inputs are finite; a program needn't handle non-finite values.
Results may differ from the reference program's by a relative error of at most 0.029.
Values may be sent and summed in bfloat16 or wider, within the bound.
A program may use at most 128 MiB of HBM per device.

```python
import math
import jax
import jax.numpy as jnp
from jax import lax

D = 8192
QH = 64
KVH = 8
HD = 128
FEAT = 8192
QPI = 192
IMGS = 2
TILES = 4
GROUPS = 4
ROWS = 4096
TILE_ROWS = 1024
IMAGES = 8
Q_ALL = 1536


def draw_group_images(key, part):
    key = jax.random.fold_in(key, 11)
    first, second, third, fourth = jax.random.split(key, 4)
    order = jax.random.permutation(first, GROUPS)
    inverse = jnp.argsort(order).astype(jnp.int32)
    shift = jax.random.randint(second, (), 1, GROUPS)
    flipped = jax.random.randint(third, (GROUPS,), 0, 2)
    swapped = jax.random.randint(fourth, (GROUPS,), 0, 2)
    source_zero = inverse
    source_one = (inverse - shift) % GROUPS
    image_zero = source_zero * 2 + flipped[source_zero]
    image_one = source_one * 2 + (1 - flipped[source_one])
    slot_first = jnp.where(swapped == 1, image_one, image_zero)
    slot_second = jnp.where(swapped == 1, image_zero, image_one)
    return jnp.stack([slot_first, slot_second], axis=1).astype(jnp.int32)


def draw_queries(key, part):
    key = jax.random.fold_in(key, 5)
    first = jax.random.fold_in(key, 0)
    values = jnp.clip(jax.random.normal(first, (Q_ALL, QH * HD), jnp.float32), -6.0, 6.0)
    return values.astype(jnp.bfloat16)


def plant(array, stream_key, smallest, top_value):
    extent = array.shape
    place = [jax.random.randint(jax.random.fold_in(stream_key, axis), (), 0, extent[axis]) for axis in range(len(extent))]
    array = array.at[tuple(place)].set(smallest)
    longest = extent.index(max(extent))
    place[longest] = (place[longest] + 1) % extent[longest]
    return array.at[tuple(place)].set(top_value)


def shard_levels(key, dims, shards, least, high):
    def one(dim, shards_of):
        steps = jax.random.uniform(jax.random.fold_in(jax.random.fold_in(key, 6), dim), (shards_of,), jnp.float32, least / len(shards), high / len(shards))
        return jnp.repeat(jnp.exp(steps), dims[dim] // shards_of).reshape((-1,) + (1,) * (len(dims) - dim - 1))

    loudness = one(*shards[0])
    for cut in shards[1:]:
        loudness = loudness * one(*cut)
    return loudness


def normal_values(stream_key, dims, width, most, cuts=(), dtype=jnp.bfloat16):
    drawn = jax.random.normal(stream_key, dims, jnp.float32) * width
    if len(cuts) > 0:
        drawn = shard_levels(stream_key, dims, cuts, -0.22, 0.18) * drawn
    return jnp.clip(drawn, min=-most, max=most).astype(dtype)


def setup_inputs(seed: int = 0) -> dict:
    seeds = jax.random.split(jax.random.key(seed), 9)
    features = normal_values(seeds[0], (IMAGES, ROWS, FEAT), 1.0, 6.0, ((0, 4), (1, 64)))
    kv_weights = normal_values(seeds[1], (2, FEAT, KVH * HD), FEAT ** -0.5, 0.0625, ((1, 32), (2, 2)))
    key_gain = jnp.clip(1.0 + 0.18 * jax.random.normal(seeds[2], (HD,), jnp.float32), 0.1, 1.9)
    queries = draw_queries(jax.random.fold_in(seeds[8], 71), 0)
    out_weight = normal_values(seeds[4], (QH * HD, D), 1.0, 6.0, ((0, 2), (1, 32)))
    attn_gate = jnp.clip(jax.random.uniform(seeds[5], (1,), jnp.float32, 0.4, 1.5), 0.4, 1.5)
    group_images = draw_group_images(jax.random.fold_in(seeds[8], 71), 0)
    tile_valid = plant(jax.random.randint(seeds[7], (IMAGES, TILES), 1, TILE_ROWS + 1), jax.random.fold_in(seeds[7], 1), 1, TILE_ROWS).astype(jnp.int32)
    return {"features": features, "kv_weights": kv_weights, "key_gain": key_gain, "queries": queries, "out_weight": out_weight, "attn_gate": attn_gate, "group_images": group_images, "tile_valid": tile_valid}


def normed_keys(raw_keys, key_gain):
    return raw_keys * lax.rsqrt(lax.optimization_barrier(jnp.mean(raw_keys * raw_keys, axis=-1, keepdims=True)) + 1e-05) * key_gain

def reference(features, kv_weights, key_gain, queries, out_weight, attn_gate, group_images, tile_valid):
    head_group = QH // KVH
    score_scale = 1.0 / math.sqrt(HD)
    row_index = jnp.arange(ROWS)
    tile_index = row_index // TILE_ROWS
    tile_place = row_index % TILE_ROWS
    flat_images = group_images.reshape(-1)

    def one_slot(slot_index):
        image = flat_images[slot_index]
        pixels = features[image]
        raw_keys = jnp.dot(pixels, kv_weights[0], preferred_element_type=jnp.float32).reshape(ROWS, KVH, HD)
        slot_keys = lax.optimization_barrier(normed_keys(raw_keys, key_gain).astype(jnp.bfloat16))
        slot_values = jnp.dot(pixels, kv_weights[1], preferred_element_type=jnp.float32).reshape(ROWS, KVH, HD).astype(jnp.bfloat16)
        row_valid = tile_place < tile_valid[image][tile_index]
        slot_queries = lax.dynamic_slice_in_dim(queries, slot_index * QPI, QPI, 0).reshape(QPI, KVH, head_group, HD)

        def one_head(head):
            head_queries = slot_queries[:, head].astype(jnp.float32)
            head_keys = slot_keys[:, head].astype(jnp.float32)
            head_values = slot_values[:, head].astype(jnp.float32)
            scores = jnp.einsum('qgd,rd->qgr', head_queries, head_keys) * score_scale
            scores = jnp.where(row_valid[None, None, :], scores, -1e+30)
            peak = lax.optimization_barrier(jnp.max(scores, axis=-1, keepdims=True))
            weights_exp = jnp.exp(scores - peak)
            totals = lax.optimization_barrier(jnp.sum(weights_exp, axis=-1))
            prob_weights = lax.optimization_barrier(weights_exp.astype(jnp.bfloat16)).astype(jnp.float32)
            summed = jnp.einsum('qgr,rd->qgd', prob_weights, head_values)
            return (summed / totals[:, :, None]).astype(jnp.bfloat16)
        per_head = lax.map(one_head, jnp.arange(KVH))
        return per_head.transpose(1, 0, 2, 3).reshape(QPI, QH * HD)
    attention = lax.map(one_slot, jnp.arange(GROUPS * IMGS)).reshape(Q_ALL, QH * HD)
    projected = jnp.dot(attention, out_weight, preferred_element_type=jnp.float32)
    return (projected * jnp.tanh(attn_gate[0])).astype(jnp.bfloat16)
```

```python
import math

import jax
import jax.numpy as jnp
from jax import lax
from jax.experimental import pallas as pl
from jax.experimental.pallas import tpu as pltpu
from jax.sharding import PartitionSpec as P

HD = 128
MESH = pl.DeviceIdType.MESH
BF = jnp.bfloat16
F32 = jnp.float32
NX, NY, NZ = 4, 4, 8
WIDE = 640
NARROW = 1024 - WIDE


def fused(
    feat, kvw, gain, queries, out_w, gate, images, counts, out,
    a_ref, relay, w_ref, p_ref, rs_relay, rs_recv, xs_ref, xk_ref, xv_ref, q_ref, pr_ref,
    o_ref, st_ref, zo_ref, zs_ref, at1, at2, ow_ref, acc_ref, cs_ref, cr_ref,
    loc_sem, f_send, f_recv, wk_send, wk_recv, wv_send, wv_recv, wx_send, wx_recv,
    rs_send, rs_rsem, x_send, x_recv, zo_send, zo_recv, zs_send, zs_recv,
    y2_send, y2_recv, z1_send, z1_recv, z2_send, z2_recv, y1_send, y1_recv, c_send, c_recv,
):
    x = lax.axis_index("group")
    img = lax.axis_index("img")
    t = lax.axis_index("tensor")
    z = img // NY
    y = img % NY
    other = 1 - t

    def ym(d):
        return (y + d + NY) % NY

    def zm(d):
        return (z + d + NZ) % NZ

    def xm(d):
        return (x + d + NX) % NX

    def to_y(d):
        return {"img": z * NY + ym(d)}

    def to_z(d):
        return {"img": zm(d) * NY + y}

    def to_x(d):
        return {"group": xm(d)}

    sibling = {"tensor": other}
    sends = []

    def remote(src, dst, ssem, rsem, where):
        return pltpu.make_async_remote_copy(
            src_ref=src, dst_ref=dst, send_sem=ssem, recv_sem=rsem,
            device_id=where, device_id_type=MESH,
        )

    def send(src, dst, ssem, rsem, where):
        copy = remote(src, dst, ssem, rsem, where)
        copy.start()
        sends.append(copy)

    def arrived(ref, sem):
        pltpu.make_async_copy(ref, ref, sem).wait()

    barrier = pltpu.get_barrier_semaphore()
    partners = [sibling] + [to_y(d) for d in (1, 2, 3)] + [to_x(d) for d in (1, 2, 3)]
    partners += [to_z(d) for d in range(1, NZ)]
    for where in partners:
        pl.semaphore_signal(barrier, inc=1, device_id=where, device_id_type=MESH)
    pl.semaphore_wait(barrier, len(partners))

    quarter = pl.ds(pl.multiple_of(x * 64, 64), 64)
    halves = (
        pl.ds(pl.multiple_of(x * 64, 64), 32),
        pl.ds(pl.multiple_of(x * 64 + 32, 32), 32),
    )

    def wk_step(s):
        for way, sign in ((0, -1), (1, 1)):
            origin = zm(sign * (s - 1))
            rows = quarter if s < 4 else halves[way]
            src = kvw.at[0, rows, :] if s == 1 else w_ref.at[0, origin, rows, :]
            send(src, w_ref.at[0, origin, rows, :], wk_send.at[way, s - 1], wk_recv.at[way, s - 1], to_z(-sign))

    def wk_wait(s):
        for way, sign in ((0, -1), (1, 1)):
            rows = quarter if s < 4 else halves[way]
            arrived(w_ref.at[0, zm(sign * s), rows, :], wk_recv.at[way, s - 1])

    v_halves = (pl.ds(0, 128), pl.ds(128, 128))

    def wv_step(s):
        for way, sign in ((0, -1), (1, 1)):
            origin = zm(sign * (s - 1))
            rows = pl.ds(0, 256) if s < 4 else v_halves[way]
            src = kvw.at[1, rows, :] if s == 1 else w_ref.at[1, origin, rows, :]
            send(src, w_ref.at[1, origin, rows, :], wv_send.at[way, s - 1], wv_recv.at[way, s - 1], to_z(-sign))

    def wv_wait(s):
        for way, sign in ((0, -1), (1, 1)):
            rows = pl.ds(0, 256) if s < 4 else v_halves[way]
            arrived(w_ref.at[1, zm(sign * s), rows, :], wv_recv.at[way, s - 1])

    wk_step(1)

    def columns(block, kind):
        return pl.ds(pl.multiple_of((block * NY + kind) * 256, 256), 256)

    def place(block):
        return pl.ds(pl.multiple_of(block * 256, 256), 256)

    def start_relays(block, carry):
        far = columns(block, ym(2))
        remote(feat.at[0, :, far], relay.at[0, :, place(block)], f_send.at[0], f_recv.at[0], to_y(1)).start()
        remote(feat.at[1, :, far], relay.at[1, :, place(block)], f_send.at[1], f_recv.at[1], to_y(-1)).start()
        return carry

    def start_direct(block, carry):
        mine = a_ref.at[y, t, :, :, place(block)]
        remote(feat.at[:, :, columns(block, ym(1))], mine, f_send.at[2], f_recv.at[2], to_y(1)).start()
        remote(feat.at[:, :, columns(block, ym(-1))], mine, f_send.at[3], f_recv.at[3], to_y(-1)).start()
        return carry

    def start_own(block, carry):
        mine = a_ref.at[y, t, :, :, place(block)]
        own = feat.at[:, :, columns(block, y)]
        remote(own, mine, f_send.at[4], f_recv.at[4], sibling).start()
        pltpu.make_async_copy(own, mine, loc_sem.at[0]).start()
        return carry

    lax.fori_loop(0, NZ, start_relays, 0)
    lax.fori_loop(0, NZ, start_direct, 0)
    wv_step(1)
    lax.fori_loop(0, NZ, start_own, 0)
    own_wk = pltpu.make_async_copy(kvw.at[0, quarter, :], w_ref.at[0, z, quarter, :], loc_sem.at[1])
    own_wk.start()
    own_wv = pltpu.make_async_copy(kvw.at[1], w_ref.at[1, z], loc_sem.at[2])
    own_wv.start()
    own_q = pltpu.make_async_copy(queries.at[:, pl.ds(pl.multiple_of(y * 1024, 1024), 1024)], q_ref, loc_sem.at[3])
    own_q.start()
    own_ow = pltpu.make_async_copy(out_w, ow_ref, loc_sem.at[4])
    own_ow.start()

    for s in (1, 2, 3):
        wk_wait(s)
        wk_step(s + 1)
    arrived(relay.at[0], f_recv.at[0])
    send(relay.at[0], a_ref.at[ym(-1), t, 0], f_send.at[5], f_recv.at[5], to_y(1))
    arrived(relay.at[1], f_recv.at[1])
    send(relay.at[1], a_ref.at[ym(1), t, 1], f_send.at[6], f_recv.at[6], to_y(-1))
    wk_wait(4)
    own_wk.wait()
    mine = w_ref.at[0, :, quarter, :]
    send(mine, mine, wx_send.at[0], wx_recv.at[0], to_x(1))
    send(mine, mine, wx_send.at[1], wx_recv.at[1], to_x(-1))
    wv_wait(1)
    wv_step(2)
    wv_wait(2)
    wv_step(3)

    def pass_to_sibling(which, slot):
        block = a_ref.at[which, t]
        send(block, block, f_send.at[slot], f_recv.at[slot], sibling)

    arrived(a_ref.at[ym(-1), t], f_recv.at[2])
    pass_to_sibling(ym(-1), 7)
    arrived(a_ref.at[ym(1), t], f_recv.at[3])
    pass_to_sibling(ym(1), 8)

    below = pl.ds(pl.multiple_of(xm(-1) * 64, 64), 64)
    above = pl.ds(pl.multiple_of(xm(1) * 64, 64), 64)
    across = pl.ds(pl.multiple_of(xm(2) * 64, 64), 64)
    arrived(w_ref.at[0, :, below, :], wx_recv.at[0])
    from_below = w_ref.at[0, pl.ds(0, 4), below, :]
    send(from_below, from_below, wx_send.at[2], wx_recv.at[2], to_x(1))
    arrived(w_ref.at[0, :, above, :], wx_recv.at[1])
    from_above = w_ref.at[0, pl.ds(4, 4), above, :]
    send(from_above, from_above, wx_send.at[3], wx_recv.at[3], to_x(-1))
    wv_wait(3)
    wv_step(4)
    arrived(a_ref.at[ym(2), t, 0], f_recv.at[5])
    arrived(a_ref.at[ym(2), t, 1], f_recv.at[6])
    pass_to_sibling(ym(2), 9)
    arrived(w_ref.at[0, pl.ds(0, 4), across, :], wx_recv.at[2])
    arrived(w_ref.at[0, pl.ds(4, 4), across, :], wx_recv.at[3])
    pltpu.make_async_copy(a_ref.at[y, t], a_ref.at[y, t], loc_sem.at[0]).wait()
    arrived(a_ref.at[y, other], f_recv.at[4])
    arrived(a_ref.at[ym(-1), other], f_recv.at[7])
    arrived(a_ref.at[ym(1), other], f_recv.at[8])
    arrived(a_ref.at[ym(2), other], f_recv.at[9])

    def project(kind):
        def rows_of(src, carry):
            part = jnp.dot(
                a_ref[src].reshape(256, 2048), w_ref[kind].reshape(2048, 512), preferred_element_type=F32
            ).astype(BF)
            for core in range(2):
                for image in range(2):
                    rows = part[core * 128 + image * 64 : core * 128 + image * 64 + 64]
                    where = pl.ds(pl.multiple_of(src * 128 + core * 64, 64), 64)
                    for head in range(4):
                        p_ref[kind, head, image, where, :] = rows[:, head * 128 : head * 128 + 128]
            return carry

        lax.fori_loop(0, NY, rows_of, 0)

    def rs_start(kind):
        ss, rr = rs_send, rs_rsem
        send(p_ref.at[kind, ym(2), 0], rs_relay.at[kind, 0], ss.at[kind, 0], rr.at[kind, 0], to_y(1))
        send(p_ref.at[kind, ym(2), 1], rs_relay.at[kind, 1], ss.at[kind, 1], rr.at[kind, 1], to_y(-1))
        send(p_ref.at[kind, ym(1), 1], rs_recv.at[kind, 0, 1], ss.at[kind, 2], rr.at[kind, 2], to_y(1))
        send(p_ref.at[kind, ym(-1), 0], rs_recv.at[kind, 1, 0], ss.at[kind, 3], rr.at[kind, 3], to_y(-1))

    def rs_middle(kind):
        ss, rr = rs_send, rs_rsem
        for way, d in ((0, 1), (1, -1)):
            arrived(rs_relay.at[kind, way], rr.at[kind, way])
            p_ref[kind, ym(d), way] = (
                p_ref[kind, ym(d), way].astype(F32) + rs_relay[kind, way].astype(F32)
            ).astype(BF)
            send(
                p_ref.at[kind, ym(d), way], rs_recv.at[kind, way, way],
                ss.at[kind, 4 + way], rr.at[kind, 4 + way], to_y(d),
            )

    def rs_finish(kind):
        rr = rs_rsem
        xr_ref = (xk_ref, xv_ref)[kind]
        arrived(rs_recv.at[kind, 0, 1], rr.at[kind, 2])
        arrived(rs_recv.at[kind, 1, 0], rr.at[kind, 3])
        arrived(rs_recv.at[kind, 0, 0], rr.at[kind, 4])
        arrived(rs_recv.at[kind, 1, 1], rr.at[kind, 5])
        both = []
        for image in range(2):
            total = (
                p_ref[kind, y, image].astype(F32)
                + rs_recv[kind, 0, image].astype(F32)
                + rs_recv[kind, 1, image].astype(F32)
            )
            if kind == 0:
                mean = jnp.mean(total * total, axis=-1, keepdims=True)
                total = total * lax.rsqrt(mean + 1e-05) * gain[...]
            both.append(total.astype(BF))
        for d in range(NX):
            group = xm(d)
            second = (images[group, 0] == 2 * x + 1) | (images[group, 1] == 2 * x + 1)
            block = jnp.where(second, both[1], both[0])
            if d == 0:
                xr_ref[x] = block
            else:
                xs_ref[kind, d - 1] = block
                send(xs_ref.at[kind, d - 1], xr_ref.at[x], x_send.at[kind, d - 1], x_recv.at[kind, d - 1], to_x(d))

    def x_wait(kind):
        xr_ref = (xk_ref, xv_ref)[kind]
        for d in range(1, NX):
            arrived(xr_ref.at[xm(-d)], x_recv.at[kind, d - 1])

    project(0)
    rs_start(0)
    wv_wait(4)
    own_wv.wait()
    project(1)
    rs_start(1)
    rs_middle(0)
    rs_middle(1)
    rs_finish(0)
    own_q.wait()
    x_wait(0)

    scale = 1.0 / math.sqrt(HD)
    lane = lax.broadcasted_iota(jnp.int32, (192, 128), 1)
    key_row = lax.broadcasted_iota(jnp.int32, (192, 512), 1)

    def scores(slot):
        image = images[x, slot]
        keys = xk_ref[image // 2]
        valid = key_row < counts[image, z // 2] - (z % 2) * 512
        rows = pl.ds(slot * 192, 192)

        def one_head(head, stats):
            q = q_ref[rows, pl.ds(pl.multiple_of(head * 128, 128), 128)]
            s = lax.dot_general(q, keys, (((1,), (1,)), ((), ())), preferred_element_type=F32) * scale
            s = jnp.where(valid, s, -1e30)
            peak = jnp.max(s, axis=-1, keepdims=True)
            e = jnp.exp(s - peak)
            total = jnp.sum(e, axis=-1, keepdims=True)
            pr_ref[slot, head] = e.astype(BF)
            return jnp.where(lane == head, peak, jnp.where(lane == head + 8, total, stats))

        st_ref[rows, :] = lax.fori_loop(0, 8, one_head, jnp.zeros((192, 128), F32))

    def weigh(slot):
        image = images[x, slot]
        values = xv_ref[image // 2]
        rows = pl.ds(slot * 192, 192)

        def one_head(head, carry):
            o = jnp.dot(pr_ref[slot, head], values, preferred_element_type=F32)
            o_ref[rows, pl.ds(pl.multiple_of(head * 128, 128), 128)] = o.astype(BF)
            return carry

        lax.fori_loop(0, 8, one_head, 0)

    scores(0)
    rs_finish(1)
    scores(1)
    x_wait(1)
    weigh(0)
    weigh(1)

    for d in range(1, NZ):
        rows = pl.ds(pl.multiple_of(zm(d) * 48, 16), 48)
        send(o_ref.at[rows, :], zo_ref.at[d], zo_send.at[d - 1], zo_recv.at[d - 1], to_z(d))
        send(st_ref.at[rows, :], zs_ref.at[d], zs_send.at[d - 1], zs_recv.at[d - 1], to_z(d))
    rows = pl.ds(pl.multiple_of(z * 48, 16), 48)
    zo_ref[0] = o_ref[rows, :]
    zs_ref[0] = st_ref[rows, :]
    for d in range(1, NZ):
        arrived(zs_ref.at[d], zs_recv.at[d - 1])
    stats = [zs_ref[d] for d in range(NZ)]
    peak = stats[0]
    for d in range(1, NZ):
        peak = jnp.maximum(peak, stats[d])
    shares = [jnp.exp(s - peak) for s in stats]
    total = jnp.zeros((48, 128), F32)
    for d in range(NZ):
        total = total + shares[d] * pltpu.roll(stats[d], 120, 1)
    sums = [jnp.zeros((48, 128), F32) for _ in range(8)]
    for d in range(NZ):
        if d > 0:
            arrived(zo_ref.at[d], zo_recv.at[d - 1])
        for head in range(8):
            sums[head] = sums[head] + zo_ref[d, :, head * 128 : head * 128 + 128].astype(F32) * shares[d][:, head : head + 1]
    for head in range(8):
        done = (sums[head] / total[:, head : head + 1]).astype(BF)
        if head * 128 < WIDE:
            at1[y, z, :, head * 128 : head * 128 + 128] = done
        else:
            at2[z, y, :, head * 128 - WIDE : head * 128 - WIDE + 128] = done

    for d in (1, 2, 3):
        send(at2.at[z, y], at2.at[z, y], y2_send.at[d - 1], y2_recv.at[d - 1], to_y(d))

    def z1_step(s):
        for way, sign in ((0, -1), (1, 1)):
            if s < 4 or way == 0:
                block = at1.at[y, zm(sign * (s - 1))]
                send(block, block, z1_send.at[way, s - 1], z1_recv.at[way, s - 1], to_z(-sign))

    def z1_wait(s):
        for way, sign in ((0, -1), (1, 1)):
            if s < 4 or way == 0:
                arrived(at1.at[y, zm(sign * s)], z1_recv.at[way, s - 1])

    def z2_block(origin, s, way):
        if s < 4:
            return at2.at[origin]
        return at2.at[origin, pl.ds(2 * way, 2)]

    def z2_step(s):
        for way, sign in ((0, -1), (1, 1)):
            block = z2_block(zm(sign * (s - 1)), s, way)
            send(block, block, z2_send.at[way, s - 1], z2_recv.at[way, s - 1], to_z(-sign))

    def z2_wait(s):
        for way, sign in ((0, -1), (1, 1)):
            arrived(z2_block(zm(sign * s), s, way), z2_recv.at[way, s - 1])

    stages = ((0,), (-1, 1), (-2, 2), (-3, 3), (4,))

    def y1_step(stage):
        for off in stages[stage]:
            block = at1.at[y, zm(off)]
            send(block, block, y1_send.at[0, off + 3], y1_recv.at[0, off + 3], to_y(1))
            send(block, block, y1_send.at[1, off + 3], y1_recv.at[1, off + 3], to_y(-1))

    def y1_pass(stage):
        for off in stages[stage]:
            way = 0 if off <= 0 else 1
            d = 1 if way == 0 else -1
            for w, dd in ((0, -1), (1, 1)):
                arrived(at1.at[ym(dd), zm(off)], y1_recv.at[w, off + 3])
            block = at1.at[ym(-d), zm(off)]
            send(block, block, y1_send.at[2, off + 3], y1_recv.at[2, off + 3], to_y(d))

    def y1_last(stage):
        for off in stages[stage]:
            arrived(at1.at[ym(2), zm(off)], y1_recv.at[2, off + 3])

    z1_step(1)
    y1_step(0)
    for d in (1, 2, 3):
        arrived(at2.at[z, ym(-d)], y2_recv.at[d - 1])
    z2_step(1)
    z1_wait(1)
    z1_step(2)
    y1_step(1)
    y1_pass(0)
    z1_wait(2)
    z1_step(3)
    y1_step(2)
    z2_wait(1)
    z2_step(2)
    z1_wait(3)
    z1_step(4)
    y1_step(3)
    y1_pass(1)
    z2_wait(2)
    z2_step(3)
    z1_wait(4)
    y1_step(4)
    y1_pass(2)
    z2_wait(3)
    z2_step(4)
    y1_pass(3)
    y1_pass(4)
    for stage in range(5):
        y1_last(stage)
    z2_wait(4)
    own_ow.wait()

    acc = jnp.zeros((384, 256), F32)
    for block in range(NY):
        acc = acc + jnp.dot(
            at1[block].reshape(384, WIDE), ow_ref[block * 1024 : block * 1024 + WIDE], preferred_element_type=F32
        )
        acc = acc + jnp.dot(
            at2[:, block].reshape(384, NARROW), ow_ref[block * 1024 + WIDE : block * 1024 + 1024],
            preferred_element_type=F32,
        )
    acc_ref[...] = acc
    cs_ref[...] = acc_ref[pl.ds(pl.multiple_of(other * 192, 64), 192), :].astype(BF)
    send(cs_ref, cr_ref, c_send, c_recv, sibling)
    mine_sum = acc_ref[pl.ds(pl.multiple_of(t * 192, 64), 192), :]
    arrived(cr_ref, c_recv)
    out[...] = ((mine_sum + cr_ref[...].astype(F32)) * jnp.tanh(gate[...])).astype(BF)

    for copy in sends:
        copy.wait_send()
    for slot in (0, 1):
        pltpu.make_async_copy(relay.at[slot], relay.at[slot], f_send.at[slot]).wait()
    for slot in (2, 3, 4):
        pltpu.make_async_copy(a_ref.at[y, t], a_ref.at[y, t], f_send.at[slot]).wait()


def local(features, kv_weights, key_gain, queries, out_weight, attn_gate, group_images, tile_valid):
    anywhere = pl.BlockSpec(memory_space=pl.ANY)
    vmem = pl.BlockSpec(memory_space=pltpu.VMEM)
    smem = pl.BlockSpec(memory_space=pltpu.SMEM)
    dma = pltpu.SemaphoreType.DMA
    return pl.pallas_call(
        fused,
        out_shape=jax.ShapeDtypeStruct((192, 256), BF),
        in_specs=[anywhere, anywhere, vmem, anywhere, anywhere, vmem, smem, smem],
        out_specs=vmem,
        scratch_shapes=[
            pltpu.VMEM((NY, 2, 2, 64, 2048), BF),
            pltpu.VMEM((2, 64, 2048), BF),
            pltpu.VMEM((2, NZ, 256, 512), BF),
            pltpu.VMEM((2, 4, 2, 512, HD), BF),
            pltpu.VMEM((2, 2, 512, HD), BF),
            pltpu.VMEM((2, 2, 2, 512, HD), BF),
            pltpu.VMEM((2, 3, 512, HD), BF),
            pltpu.VMEM((NX, 512, HD), BF),
            pltpu.VMEM((NX, 512, HD), BF),
            pltpu.VMEM((384, 1024), BF),
            pltpu.VMEM((2, 8, 192, 512), BF),
            pltpu.VMEM((384, 1024), BF),
            pltpu.VMEM((384, 128), F32),
            pltpu.VMEM((NZ, 48, 1024), BF),
            pltpu.VMEM((NZ, 48, 128), F32),
            pltpu.VMEM((NY, NZ, 48, WIDE), BF),
            pltpu.VMEM((NZ, NY, 48, NARROW), BF),
            pltpu.VMEM((4096, 256), BF),
            pltpu.VMEM((384, 256), F32),
            pltpu.VMEM((192, 256), BF),
            pltpu.VMEM((192, 256), BF),
            dma((5,)),
            dma((10,)), dma((10,)),
            dma((2, 4)), dma((2, 4)),
            dma((2, 4)), dma((2, 4)),
            dma((4,)), dma((4,)),
            dma((2, 6)), dma((2, 6)),
            dma((2, 3)), dma((2, 3)),
            dma((7,)), dma((7,)), dma((7,)), dma((7,)),
            dma((3,)), dma((3,)),
            dma((2, 4)), dma((2, 4)),
            dma((2, 4)), dma((2, 4)),
            dma((3, 8)), dma((3, 8)),
            dma, dma,
        ],
        compiler_params=pltpu.CompilerParams(
            collective_id=0, has_side_effects=True, vmem_limit_bytes=56 * 1024 * 1024
        ),
        name="fused",
    )(
        features, kv_weights, key_gain.reshape(1, HD), queries, out_weight,
        attn_gate.reshape(1, 1), group_images, tile_valid,
    )


def solution(mesh):
    placed = (
        P("group", ("img", "tensor"), None),
        P(None, "img", "tensor"),
        P(),
        P("group", "tensor"),
        P("tensor", "img"),
        P(),
        P(),
        P(),
    )
    return jax.shard_map(
        local, mesh=mesh, in_specs=placed, out_specs=P(("group", "tensor"), "img"), check_vma=False
    )
```

```python
import math

import jax
import jax.numpy as jnp
from jax import lax
from jax.experimental import pallas as pl
from jax.experimental.pallas import tpu as pltpu
from jax.sharding import PartitionSpec as P

HD = 128
MESH = pl.DeviceIdType.MESH
BF = jnp.bfloat16
F32 = jnp.float32
NX, NY, NZ = 4, 4, 8
WIDE = 512
NARROW = 1024 - WIDE


def fused(
    feat, kvw, gain, queries, out_w, gate, images_hbm, counts_hbm, out,
    images, counts, a_ref, w_ref, p_ref, rs_relay, rs_recv, xs_ref, xk_ref, xv_ref, ks_ref, vs_ref, kb_ref, vb_ref,
    q_ref, pr_ref, o_ref, st_ref, zo_ref, zs_ref, at1, at2, ow_ref, acc_ref, cs_ref, cr_ref,
    loc_sem, f_send, f_recv, c_fsend, c_frecv, w_send, w_recv, wx_send, wx_recv,
    rs_send, rs_rsem, x_send, x_recv, pair_send, pair_recv, zo_send, zo_recv, zs_send, zs_recv,
    y2_send, y2_recv, z1_send, z1_recv, z2_send, z2_recv, y1_send, y1_recv, c_send, c_recv,
):
    x = lax.axis_index("group")
    img = lax.axis_index("img")
    t = lax.axis_index("tensor")
    z = img // NY
    y = img % NY
    other = 1 - t
    slot = z % 2

    def ym(d):
        return (y + d + NY) % NY

    def zm(d):
        return (z + d + NZ) % NZ

    def xm(d):
        return (x + d + NX) % NX

    def to_y(d):
        return {"img": z * NY + ym(d)}

    def to_z(d):
        return {"img": zm(d) * NY + y}

    def to_x(d):
        return {"group": xm(d)}

    sibling = {"tensor": other}
    partner = {"img": (z + 1 - 2 * slot) * NY + y}
    sends = []

    def remote(src, dst, ssem, rsem, where):
        return pltpu.make_async_remote_copy(
            src_ref=src, dst_ref=dst, send_sem=ssem, recv_sem=rsem,
            device_id=where, device_id_type=MESH,
        )

    def send(src, dst, ssem, rsem, where):
        copy = remote(src, dst, ssem, rsem, where)
        copy.start()
        sends.append(copy)

    def arrived(ref, sem):
        pltpu.make_async_copy(ref, ref, sem).wait()

    locals_ = []

    def fetch(src, dst, sem):
        copy = pltpu.make_async_copy(src, dst, sem)
        copy.start()
        locals_.append(copy)

    third = (
        pl.ds(pl.multiple_of(128 + x * 32, 32), 32),
        pl.ds(pl.multiple_of(128 + x * 32, 16), 16),
        pl.ds(pl.multiple_of(128 + x * 32 + 16, 16), 16),
    )

    def columns(block, kind):
        return pl.ds(pl.multiple_of((block * NY + kind) * 256, 256), 256)

    def place(block):
        return pl.ds(pl.multiple_of(block * 256, 256), 256)

    def fetch_own(block, carry):
        own = feat.at[:, :, columns(block, y)]
        pltpu.make_async_copy(own, a_ref.at[y, t, :, :, place(block)], loc_sem.at[0]).start()
        return carry

    lax.fori_loop(0, NZ, fetch_own, 0)
    fetch(images_hbm, images, loc_sem.at[1])
    fetch(counts_hbm, counts, loc_sem.at[2])
    for kind in range(2):
        fetch(kvw.at[kind, pl.ds(0, 128), :], w_ref.at[kind, z, pl.ds(0, 128), :], loc_sem.at[3 + kind])
        fetch(kvw.at[kind, third[0], :], w_ref.at[kind, z, third[0], :], loc_sem.at[5 + kind])
    q_rows = pl.ds(pl.multiple_of(slot * 192, 64), 192)
    fetch(queries.at[q_rows, pl.ds(pl.multiple_of(y * 1024, 1024), 1024)], q_ref, loc_sem.at[7])
    fetch(out_w, ow_ref, loc_sem.at[8])

    barrier = pltpu.get_barrier_semaphore()
    partners = [sibling] + [to_y(d) for d in (1, 2, 3)] + [to_x(d) for d in (1, 2, 3)]
    partners += [to_z(d) for d in (1, 2, 4, 6, 7)]
    for where in partners:
        pl.semaphore_signal(barrier, inc=1, device_id=where, device_id_type=MESH)
    pl.semaphore_wait(barrier, len(partners))

    def w_parts(s, way):
        if s < 4:
            return (pl.ds(0, 128), third[0])
        return (pl.ds(64 * way, 64), third[1 + way])

    def w_step(kind, s):
        for way, sign in ((0, -1), (1, 1)):
            origin = zm(sign * (s - 1))
            for part, rows in enumerate(w_parts(s, way)):
                src = kvw.at[kind, rows, :] if s == 1 else w_ref.at[kind, origin, rows, :]
                k = (kind * 2 + way) * 8 + (s - 1) * 2 + part
                send(src, w_ref.at[kind, origin, rows, :], w_send.at[k], w_recv.at[k], to_z(-sign))

    def w_wait(kind, s):
        for way, sign in ((0, -1), (1, 1)):
            for part, rows in enumerate(w_parts(s, way)):
                k = (kind * 2 + way) * 8 + (s - 1) * 2 + part
                arrived(w_ref.at[kind, zm(sign * s), rows, :], w_recv.at[k])

    def w_share(kind, offsets):
        for off in offsets:
            dst = w_ref.at[kind, zm(off), third[0], :]
            src = kvw.at[kind, third[0], :] if off == 0 else dst
            for d in (2, 1, 3):
                remote(src, dst, wx_send.at[kind, d - 1], wx_recv.at[kind, d - 1], to_x(d)).start()

    def w_shared(kind):
        for d in (1, 2, 3):
            rows = pl.ds(pl.multiple_of(128 + xm(-d) * 32, 32), 32)
            arrived(w_ref.at[kind, :, rows, :], wx_recv.at[kind, d - 1])

    def start_image(image):
        def start(block, carry):
            for d in (2, 1, 3):
                remote(
                    feat.at[image, :, columns(block, ym(d))], a_ref.at[y, t, image, :, place(block)],
                    f_send.at[image, d - 1], f_recv.at[image, d - 1], to_y(d),
                ).start()
            return carry

        lax.fori_loop(0, NZ, start, 0)

    def start_own(block, carry):
        own = feat.at[:, :, columns(block, y)]
        remote(own, a_ref.at[y, t, :, :, place(block)], c_fsend.at[6], c_frecv.at[6], sibling).start()
        return carry

    def pass_image(image):
        for d in (1, 2, 3):
            block = a_ref.at[ym(-d), t, image]
            arrived(block, f_recv.at[image, d - 1])
            k = image * 3 + d - 1
            send(block, block, c_fsend.at[k], c_frecv.at[k], sibling)

    w_step(0, 1)
    start_image(0)
    w_share(0, (0,))
    w_step(1, 1)
    start_image(1)
    w_share(1, (0,))
    lax.fori_loop(0, NZ, start_own, 0)

    for s in (1, 2, 3):
        for kind in range(2):
            w_wait(kind, s)
            w_step(kind, s + 1)
            w_share(kind, (-s, s))
        if s == 2:
            pass_image(0)
    w_wait(0, 4)
    w_share(0, (4,))
    w_wait(1, 4)
    w_share(1, (4,))
    pass_image(1)

    arrived(a_ref.at[y, t], loc_sem.at[0])
    for copy in locals_:
        copy.wait()
    arrived(a_ref.at[y, other], c_frecv.at[6])
    for image in range(2):
        for d in (1, 2, 3):
            arrived(a_ref.at[ym(-d), other, image], c_frecv.at[image * 3 + d - 1])

    def project(kind):
        def rows_of(src, carry):
            part = jnp.dot(
                a_ref[src].reshape(256, 2048), w_ref[kind].reshape(2048, 512), preferred_element_type=F32
            ).astype(BF)
            for core in range(2):
                for image in range(2):
                    rows = part[core * 128 + image * 64 : core * 128 + image * 64 + 64]
                    where = pl.ds(pl.multiple_of(src * 128 + core * 64, 64), 64)
                    for head in range(4):
                        p_ref[kind, head, image, where, :] = rows[:, head * 128 : head * 128 + 128]
            return carry

        lax.fori_loop(0, NY, rows_of, 0)

    def rs_start(kind):
        ss, rr = rs_send, rs_rsem
        send(p_ref.at[kind, ym(2), 0], rs_relay.at[kind, 0], ss.at[kind, 0], rr.at[kind, 0], to_y(1))
        send(p_ref.at[kind, ym(2), 1], rs_relay.at[kind, 1], ss.at[kind, 1], rr.at[kind, 1], to_y(-1))
        send(p_ref.at[kind, ym(1), 1], rs_recv.at[kind, 0, 1], ss.at[kind, 2], rr.at[kind, 2], to_y(1))
        send(p_ref.at[kind, ym(-1), 0], rs_recv.at[kind, 1, 0], ss.at[kind, 3], rr.at[kind, 3], to_y(-1))

    def rs_middle(kind):
        ss, rr = rs_send, rs_rsem
        for way, d in ((0, 1), (1, -1)):
            arrived(rs_relay.at[kind, way], rr.at[kind, way])
            p_ref[kind, ym(d), way] = (
                p_ref[kind, ym(d), way].astype(F32) + rs_relay[kind, way].astype(F32)
            ).astype(BF)
            send(
                p_ref.at[kind, ym(d), way], rs_recv.at[kind, way, way],
                ss.at[kind, 4 + way], rr.at[kind, 4 + way], to_y(d),
            )

    def rs_finish(kind):
        rr = rs_rsem
        xr_ref = (xk_ref, xv_ref)[kind]
        arrived(rs_recv.at[kind, 0, 1], rr.at[kind, 2])
        arrived(rs_recv.at[kind, 1, 0], rr.at[kind, 3])
        arrived(rs_recv.at[kind, 0, 0], rr.at[kind, 4])
        arrived(rs_recv.at[kind, 1, 1], rr.at[kind, 5])
        both = []
        for image in range(2):
            total = (
                p_ref[kind, y, image].astype(F32)
                + rs_recv[kind, 0, image].astype(F32)
                + rs_recv[kind, 1, image].astype(F32)
            )
            if kind == 0:
                mean = jnp.mean(total * total, axis=-1, keepdims=True)
                total = total * lax.rsqrt(mean + 1e-05) * gain[...]
            both.append(total.astype(BF))
        for d in (2, 1, 3, 0):
            group = xm(d)
            second = (images[0, group] == 2 * x + 1) | (images[1, group] == 2 * x + 1)
            block = jnp.where(second, both[1], both[0])
            if d == 0:
                xr_ref[x] = block
            else:
                xs_ref[kind, d - 1] = block
                send(xs_ref.at[kind, d - 1], xr_ref.at[x], x_send.at[kind, d - 1], x_recv.at[kind, d - 1], to_x(d))

    def pair(kind):
        xr_ref = (xk_ref, xv_ref)[kind]
        out_ref = (ks_ref, vs_ref)[kind]
        both_ref = (kb_ref, vb_ref)[kind]
        for d in range(1, NX):
            arrived(xr_ref.at[xm(-d)], x_recv.at[kind, d - 1])
        out_ref[...] = xr_ref[images[1 - slot, x] // 2]
        send(out_ref, both_ref.at[pl.ds(512, 512)], pair_send.at[kind], pair_recv.at[kind], partner)
        both_ref[0:512] = xr_ref[images[slot, x] // 2]

    def paired(kind):
        both_ref = (kb_ref, vb_ref)[kind]
        arrived(both_ref.at[pl.ds(512, 512)], pair_recv.at[kind])

    w_shared(0)
    project(0)
    rs_start(0)
    w_shared(1)
    project(1)
    rs_start(1)
    rs_middle(0)
    rs_middle(1)
    rs_finish(0)
    pair(0)
    rs_finish(1)
    paired(0)

    image = images[slot, x]
    scale = 1.0 / math.sqrt(HD)
    lane = lax.broadcasted_iota(jnp.int32, (192, 128), 1)
    key_row = (lax.broadcasted_iota(jnp.int32, (192, 1024), 1) + slot * 512) % 1024
    valid = key_row < counts[z // 2, image]

    def score_head(head, stats):
        q = q_ref[:, pl.ds(pl.multiple_of(head * 128, 128), 128)]
        s = lax.dot_general(q, kb_ref[...], (((1,), (1,)), ((), ())), preferred_element_type=F32) * scale
        s = jnp.where(valid, s, -1e30)
        peak = jnp.max(s, axis=-1, keepdims=True)
        e = jnp.exp(s - peak)
        total = jnp.sum(e, axis=-1, keepdims=True)
        pr_ref[head] = e.astype(BF)
        return jnp.where(lane == head, peak, jnp.where(lane == head + 8, total, stats))

    st_ref[...] = lax.fori_loop(0, 8, score_head, jnp.zeros((192, 128), F32))

    def share_of(d):
        return pl.ds(pl.multiple_of(zm(d) // 2 * 48, 16), 48)

    for k, d in enumerate((2, 4, 6)):
        send(st_ref.at[share_of(d), :], zs_ref.at[k + 1], zs_send.at[k], zs_recv.at[k], to_z(d))
    zs_ref[0] = st_ref[share_of(0), :]

    pair(1)
    paired(1)

    def weigh_head(head, carry):
        o = jnp.dot(pr_ref[head], vb_ref[...], preferred_element_type=F32)
        o_ref[:, pl.ds(pl.multiple_of(head * 128, 128), 128)] = o.astype(BF)
        return carry

    lax.fori_loop(0, 8, weigh_head, 0)
    for k, d in enumerate((2, 4, 6)):
        send(o_ref.at[share_of(d), :], zo_ref.at[k + 1], zo_send.at[k], zo_recv.at[k], to_z(d))
    zo_ref[0] = o_ref[share_of(0), :]
    for k in range(3):
        arrived(zs_ref.at[k + 1], zs_recv.at[k])
    stats = [zs_ref[k] for k in range(4)]
    peak = jnp.maximum(jnp.maximum(stats[0], stats[1]), jnp.maximum(stats[2], stats[3]))
    shares = [jnp.exp(s - peak) for s in stats]
    total = jnp.zeros((48, 128), F32)
    for k in range(4):
        total = total + shares[k] * pltpu.roll(stats[k], 120, 1)
    for k in range(3):
        arrived(zo_ref.at[k + 1], zo_recv.at[k])
    for head in range(8):
        sums = jnp.zeros((48, 128), F32)
        for k in range(4):
            sums = sums + zo_ref[k, :, head * 128 : head * 128 + 128].astype(F32) * shares[k][:, head : head + 1]
        done = (sums / total[:, head : head + 1]).astype(BF)
        if head * 128 < WIDE:
            at1[y, z, :, head * 128 : head * 128 + 128] = done
        else:
            at2[z, y, :, head * 128 - WIDE : head * 128 - WIDE + 128] = done

    def z1_step(s):
        for way, sign in ((0, -1), (1, 1)):
            if s < 4 or way == 0:
                block = at1.at[y, zm(sign * (s - 1))]
                send(block, block, z1_send.at[way, s - 1], z1_recv.at[way, s - 1], to_z(-sign))

    def z1_wait(s):
        for way, sign in ((0, -1), (1, 1)):
            if s < 4 or way == 0:
                arrived(at1.at[y, zm(sign * s)], z1_recv.at[way, s - 1])

    def z2_step(s, c):
        for way, sign in ((0, -1), (1, 1)):
            if s < 4 or way == c % 2:
                block = at2.at[zm(sign * (s - 1)), ym(-c)]
                k = (c * 2 + way) * 4 + s - 1
                send(block, block, z2_send.at[k], z2_recv.at[k], to_z(-sign))

    def z2_wait(s, c):
        for way, sign in ((0, -1), (1, 1)):
            if s < 4 or way == c % 2:
                k = (c * 2 + way) * 4 + s - 1
                arrived(at2.at[zm(sign * s), ym(-c)], z2_recv.at[k])

    def y1_step(offsets):
        for off in offsets:
            block = at1.at[y, zm(off)]
            for d in (2, 1, 3):
                k = (d - 1) * 8 + off + 3
                send(block, block, y1_send.at[k], y1_recv.at[k], to_y(d))

    z1_step(1)
    for d in (2, 1, 3):
        send(at2.at[z, y], at2.at[z, y], y2_send.at[d - 1], y2_recv.at[d - 1], to_y(d))
    z2_step(1, 0)
    y1_step((0,))
    for c in (1, 3, 2):
        arrived(at2.at[z, ym(-c)], y2_recv.at[c - 1])
        z2_step(1, c)
    for s in (1, 2, 3):
        z1_wait(s)
        z1_step(s + 1)
        y1_step((-s, s))
        for c in (0, 1, 3, 2):
            z2_wait(s, c)
            z2_step(s + 1, c)
    z1_wait(4)
    y1_step((4,))
    for c in (0, 1, 3, 2):
        z2_wait(4, c)
    for off in range(-3, 5):
        for d in (1, 2, 3):
            arrived(at1.at[ym(-d), zm(off)], y1_recv.at[(d - 1) * 8 + off + 3])

    acc = jnp.zeros((384, 256), F32)
    for block in range(NY):
        acc = acc + jnp.dot(
            at1[block].reshape(384, WIDE), ow_ref[block * 1024 : block * 1024 + WIDE], preferred_element_type=F32
        )
        acc = acc + jnp.dot(
            at2[:, block].reshape(384, NARROW), ow_ref[block * 1024 + WIDE : block * 1024 + 1024],
            preferred_element_type=F32,
        )
    acc_ref[...] = acc.reshape(4, 2, 48, 256)
    cs_ref[...] = acc_ref[:, other].reshape(192, 256).astype(BF)
    send(cs_ref, cr_ref, c_send, c_recv, sibling)
    mine_sum = acc_ref[:, t].reshape(192, 256)
    arrived(cr_ref, c_recv)
    out[...] = ((mine_sum + cr_ref[...].astype(F32)) * jnp.tanh(gate[...])).astype(BF)

    for copy in sends:
        copy.wait_send()
    for kind in range(2):
        for d in (1, 2, 3):
            arrived(w_ref.at[kind, :, third[0], :], wx_send.at[kind, d - 1])
            arrived(a_ref.at[y, t, kind], f_send.at[kind, d - 1])
    arrived(a_ref.at[y, t], c_fsend.at[6])


def local(features, kv_weights, key_gain, queries, out_weight, attn_gate, group_images, tile_valid):
    anywhere = pl.BlockSpec(memory_space=pl.ANY)
    vmem = pl.BlockSpec(memory_space=pltpu.VMEM)
    smem = pl.BlockSpec(memory_space=pltpu.SMEM)
    dma = pltpu.SemaphoreType.DMA
    return pl.pallas_call(
        fused,
        out_shape=jax.ShapeDtypeStruct((192, 256), BF),
        in_specs=[anywhere, anywhere, vmem, anywhere, anywhere, vmem, anywhere, anywhere],
        out_specs=vmem,
        scratch_shapes=[
            pltpu.SMEM((2, 4), jnp.int32),
            pltpu.SMEM((4, 8), jnp.int32),
            pltpu.VMEM((NY, 2, 2, 64, 2048), BF),
            pltpu.VMEM((2, NZ, 256, 512), BF),
            pltpu.VMEM((2, 4, 2, 512, HD), BF),
            pltpu.VMEM((2, 2, 512, HD), BF),
            pltpu.VMEM((2, 2, 2, 512, HD), BF),
            pltpu.VMEM((2, 3, 512, HD), BF),
            pltpu.VMEM((NX, 512, HD), BF),
            pltpu.VMEM((NX, 512, HD), BF),
            pltpu.VMEM((512, HD), BF),
            pltpu.VMEM((512, HD), BF),
            pltpu.VMEM((1024, HD), BF),
            pltpu.VMEM((1024, HD), BF),
            pltpu.VMEM((192, 1024), BF),
            pltpu.VMEM((8, 192, 1024), BF),
            pltpu.VMEM((192, 1024), BF),
            pltpu.VMEM((192, 128), F32),
            pltpu.VMEM((4, 48, 1024), BF),
            pltpu.VMEM((4, 48, 128), F32),
            pltpu.VMEM((NY, NZ, 48, WIDE), BF),
            pltpu.VMEM((NZ, NY, 48, NARROW), BF),
            pltpu.VMEM((4096, 256), BF),
            pltpu.VMEM((4, 2, 48, 256), F32),
            pltpu.VMEM((192, 256), BF),
            pltpu.VMEM((192, 256), BF),
            dma((9,)),
            dma((2, 3)), dma((2, 3)),
            dma((7,)), dma((7,)),
            dma((32,)), dma((32,)),
            dma((2, 3)), dma((2, 3)),
            dma((2, 6)), dma((2, 6)),
            dma((2, 3)), dma((2, 3)),
            dma((2,)), dma((2,)),
            dma((3,)), dma((3,)), dma((3,)), dma((3,)),
            dma((3,)), dma((3,)),
            dma((2, 4)), dma((2, 4)),
            dma((32,)), dma((32,)),
            dma((24,)), dma((24,)),
            dma, dma,
        ],
        compiler_params=pltpu.CompilerParams(
            collective_id=0, has_side_effects=True, vmem_limit_bytes=56 * 1024 * 1024
        ),
        name="fused",
    )(
        features, kv_weights, key_gain.reshape(1, HD), queries, out_weight,
        attn_gate.reshape(1, 1), group_images.T, tile_valid.T,
    )


def solution(mesh):
    placed = (
        P("group", ("img", "tensor"), None),
        P(None, "img", "tensor"),
        P(),
        P("group", "tensor"),
        P("tensor", "img"),
        P(),
        P(),
        P(),
    )
    return jax.shard_map(
        local, mesh=mesh, in_specs=placed, out_specs=P(("group", "tensor"), "img"), check_vma=False
    )
```

```python
import math

import jax
import jax.numpy as jnp
from jax import lax
from jax.experimental import pallas as pl
from jax.experimental.pallas import tpu as pltpu
from jax.sharding import PartitionSpec as P

HD = 128
MESH = pl.DeviceIdType.MESH
BF = jnp.bfloat16
F32 = jnp.float32
NX, NY, NZ = 4, 4, 8
WIDE = 512
NARROW = 1024 - WIDE


def fused(
    feat, kvw, gain, queries, out_w, gate, images_hbm, counts_hbm, out,
    images, counts, a_ref, w_ref, p_ref, rs_relay, rs_recv, xs_ref, xk0_ref, xk1_ref, xv0_ref, xv1_ref, ps_ref, kb_ref, vb_ref,
    q_ref, pr_ref, o_ref, st_ref, zo_ref, zs_ref, at1, at2, ow_ref, acc_ref, cs_ref, cr_ref,
    loc_sem, f_send, f_recv, c_fsend, c_frecv, w_send, w_recv, wx_send, wx_recv,
    rs_send, rs_rsem, x_send, x_recv, pair_send, pair_recv, zo_send, zo_recv, zs_send, zs_recv,
    y2_send, y2_recv, z1_send, z1_recv, z2_send, z2_recv, y1_send, y1_recv, c_send, c_recv,
):
    x = lax.axis_index("group")
    img = lax.axis_index("img")
    t = lax.axis_index("tensor")
    z = img // NY
    y = img % NY
    other = 1 - t
    slot = z % 2

    def ym(d):
        return (y + d + NY) % NY

    def zm(d):
        return (z + d + NZ) % NZ

    def xm(d):
        return (x + d + NX) % NX

    def to_y(d):
        return {"img": z * NY + ym(d)}

    def to_z(d):
        return {"img": zm(d) * NY + y}

    def to_x(d):
        return {"group": xm(d)}

    sibling = {"tensor": other}
    partner = {"img": (z + 1 - 2 * slot) * NY + y}
    sends = []

    def remote(src, dst, ssem, rsem, where):
        return pltpu.make_async_remote_copy(
            src_ref=src, dst_ref=dst, send_sem=ssem, recv_sem=rsem,
            device_id=where, device_id_type=MESH,
        )

    def send(src, dst, ssem, rsem, where):
        copy = remote(src, dst, ssem, rsem, where)
        copy.start()
        sends.append(copy)

    def arrived(ref, sem):
        pltpu.make_async_copy(ref, ref, sem).wait()

    locals_ = []

    def fetch(src, dst, sem):
        copy = pltpu.make_async_copy(src, dst, sem)
        copy.start()
        locals_.append(copy)

    third = (
        pl.ds(pl.multiple_of(128 + x * 32, 32), 32),
        pl.ds(pl.multiple_of(128 + x * 32, 16), 16),
        pl.ds(pl.multiple_of(128 + x * 32 + 16, 16), 16),
    )

    def columns(block, kind):
        return pl.ds(pl.multiple_of((block * NY + kind) * 256, 256), 256)

    def place(block):
        return pl.ds(pl.multiple_of(block * 256, 256), 256)

    def fetch_own(block, carry):
        for half in range(2):
            own = feat.at[:, pl.ds(half * 32, 32), columns(block, y)]
            pltpu.make_async_copy(own, a_ref.at[half, y, t, :, :, place(block)], loc_sem.at[0]).start()
        return carry

    lax.fori_loop(0, NZ, fetch_own, 0)
    fetch(images_hbm, images, loc_sem.at[1])
    fetch(counts_hbm, counts, loc_sem.at[2])
    for kind in range(2):
        fetch(kvw.at[kind, pl.ds(0, 128), :], w_ref.at[kind, z, pl.ds(0, 128), :], loc_sem.at[3 + kind])
        fetch(kvw.at[kind, third[0], :], w_ref.at[kind, z, third[0], :], loc_sem.at[5 + kind])
    q_rows = pl.ds(pl.multiple_of(slot * 192, 64), 192)
    fetch(queries.at[q_rows, pl.ds(pl.multiple_of(y * 1024, 1024), 1024)], q_ref, loc_sem.at[7])
    fetch(out_w, ow_ref, loc_sem.at[8])

    barrier = pltpu.get_barrier_semaphore()
    partners = [sibling] + [to_y(d) for d in (1, 2, 3)] + [to_x(d) for d in (1, 2, 3)]
    partners += [to_z(d) for d in (1, 2, 4, 6, 7)]
    for where in partners:
        pl.semaphore_signal(barrier, inc=1, device_id=where, device_id_type=MESH)
    pl.semaphore_wait(barrier, len(partners))

    def w_parts(s, way):
        if s < 4:
            return (third[0], pl.ds(0, 64), pl.ds(64, 64))
        return (third[1 + way], pl.ds(64 * way, 64))

    def w_start(kind, s, way, part):
        rows = w_parts(s, way)[part]
        sign = 2 * way - 1
        origin = zm(sign * (s - 1))
        src = kvw.at[kind, rows, :] if s == 1 else w_ref.at[kind, origin, rows, :]
        k = ((kind * 2 + way) * 4 + s - 1) * 3 + part
        send(src, w_ref.at[kind, origin, rows, :], w_send.at[k], w_recv.at[k], to_z(-sign))

    def w_begin(kind):
        for part in range(3):
            for way in range(2):
                w_start(kind, 1, way, part)
        w_share(kind, (0,))

    def w_turn(kind, s):
        for part in range(3):
            for way in range(2):
                rows = w_parts(s, way)
                if part < len(rows):
                    k = ((kind * 2 + way) * 4 + s - 1) * 3 + part
                    arrived(w_ref.at[kind, zm((2 * way - 1) * s), rows[part], :], w_recv.at[k])
                if s < 3 or (s == 3 and (part == 0 or part == 1 + way)):
                    w_start(kind, s + 1, way, min(part, 1) if s == 3 else part)
            if part == 0:
                w_share(kind, (-s, s) if s < 4 else (4,))

    def w_share(kind, offsets):
        for off in offsets:
            dst = w_ref.at[kind, zm(off), third[0], :]
            src = kvw.at[kind, third[0], :] if off == 0 else dst
            for d in (2, 1, 3):
                remote(src, dst, wx_send.at[kind, d - 1], wx_recv.at[kind, d - 1], to_x(d)).start()

    def w_shared(kind):
        for d in (1, 2, 3):
            rows = pl.ds(pl.multiple_of(128 + xm(-d) * 32, 32), 32)
            arrived(w_ref.at[kind, :, rows, :], wx_recv.at[kind, d - 1])

    def start_half(half):
        def start(block, carry):
            for d in (2, 1, 3):
                remote(
                    feat.at[:, pl.ds(half * 32, 32), columns(block, ym(d))],
                    a_ref.at[half, y, t, :, :, place(block)],
                    f_send.at[half, d - 1], f_recv.at[half, d - 1], to_y(d),
                ).start()
            return carry

        lax.fori_loop(0, NZ, start, 0)

    def start_own(block, carry):
        for half in range(2):
            own = feat.at[:, pl.ds(half * 32, 32), columns(block, y)]
            remote(own, a_ref.at[half, y, t, :, :, place(block)], c_fsend.at[6], c_frecv.at[6], sibling).start()
        return carry

    def pass_half(half):
        for d in (1, 2, 3):
            block = a_ref.at[half, ym(-d), t]
            arrived(block, f_recv.at[half, d - 1])
            k = half * 3 + d - 1
            send(block, block, c_fsend.at[k], c_frecv.at[k], sibling)

    def project(kind, half, core):
        rows = a_ref[half, :, core].reshape(256, 2048)
        part = jnp.dot(rows, w_ref[kind].reshape(2048, 512), preferred_element_type=F32).astype(BF)
        for src in range(4):
            for image in range(2):
                first = src * 64 + image * 32
                where = pl.ds(pl.multiple_of(src * 64 + core * 32, 32), 32)
                for head in range(4):
                    p_ref[kind, half, head, image, where, :] = part[first : first + 32, head * 128 : head * 128 + 128]

    def siblings_rows(half):
        if half == 0:
            arrived(a_ref.at[:, y, other], c_frecv.at[6])
        for d in (1, 2, 3):
            arrived(a_ref.at[half, ym(-d), other], c_frecv.at[half * 3 + d - 1])

    def rs_start(kind, half):
        p, ss, rr = p_ref.at[kind, half], rs_send.at[kind * 2 + half], rs_rsem.at[kind * 2 + half]
        got, via = rs_recv.at[kind, half], rs_relay.at[kind, half]
        send(p.at[ym(2), 0], via.at[0], ss.at[0], rr.at[0], to_y(1))
        send(p.at[ym(2), 1], via.at[1], ss.at[1], rr.at[1], to_y(-1))
        send(p.at[ym(1), 1], got.at[0, 1], ss.at[2], rr.at[2], to_y(1))
        send(p.at[ym(-1), 0], got.at[1, 0], ss.at[3], rr.at[3], to_y(-1))

    def rs_middle(kind, half):
        p, ss, rr = p_ref.at[kind, half], rs_send.at[kind * 2 + half], rs_rsem.at[kind * 2 + half]
        got, via = rs_recv.at[kind, half], rs_relay.at[kind, half]
        for way, d in ((0, 1), (1, -1)):
            arrived(via.at[way], rr.at[way])
            p[ym(d), way] = (p[ym(d), way].astype(F32) + via[way].astype(F32)).astype(BF)
            send(p.at[ym(d), way], got.at[way, way], ss.at[4 + way], rr.at[4 + way], to_y(d))

    x_refs = (xk0_ref, xk1_ref, xv0_ref, xv1_ref)

    def rs_finish(kind, half):
        n = kind * 2 + half
        p, rr, got, xr_ref = p_ref.at[kind, half], rs_rsem.at[n], rs_recv.at[kind, half], x_refs[n]
        arrived(got.at[0, 1], rr.at[2])
        arrived(got.at[1, 0], rr.at[3])
        arrived(got.at[0, 0], rr.at[4])
        arrived(got.at[1, 1], rr.at[5])
        both = []
        for image in range(2):
            total = p[y, image].astype(F32) + got[0, image].astype(F32) + got[1, image].astype(F32)
            if kind == 0:
                mean = jnp.mean(total * total, axis=-1, keepdims=True)
                total = total * lax.rsqrt(mean + 1e-05) * gain[...]
            both.append(total.astype(BF))
        for d in (2, 1, 3, 0):
            group = xm(d)
            second = (images[0, group] == 2 * x + 1) | (images[1, group] == 2 * x + 1)
            block = jnp.where(second, both[1], both[0])
            if d == 0:
                xr_ref[x] = block
            else:
                xs_ref[n, d - 1] = block
                send(xs_ref.at[n, d - 1], xr_ref.at[x], x_send.at[n, d - 1], x_recv.at[n, d - 1], to_x(d))

    def pair(kind, half):
        n = kind * 2 + half
        xr_ref, both_ref = x_refs[n], (kb_ref, vb_ref)[kind]
        for d in range(1, NX):
            arrived(xr_ref.at[xm(-d)], x_recv.at[n, d - 1])
        ps_ref[n] = xr_ref[images[1 - slot, x] // 2]
        send(ps_ref.at[n], both_ref.at[pl.ds(512 + half * 256, 256)], pair_send.at[n], pair_recv.at[n], partner)
        both_ref[half * 256 : half * 256 + 256] = xr_ref[images[slot, x] // 2]

    def paired(kind):
        both_ref = (kb_ref, vb_ref)[kind]
        for half in range(2):
            arrived(both_ref.at[pl.ds(512 + half * 256, 256)], pair_recv.at[kind * 2 + half])

    w_begin(0)
    start_half(0)
    start_half(1)
    lax.fori_loop(0, NZ, start_own, 0)
    w_turn(0, 1)
    w_begin(1)
    w_turn(0, 2)
    w_turn(1, 1)
    pass_half(0)
    w_turn(0, 3)
    w_turn(1, 2)
    w_turn(0, 4)
    arrived(a_ref.at[:, y, t], loc_sem.at[0])
    for copy in locals_:
        copy.wait()
    w_shared(0)
    project(0, 0, t)
    siblings_rows(0)
    project(0, 0, other)
    rs_start(0, 0)
    w_turn(1, 3)
    pass_half(1)
    rs_middle(0, 0)
    w_turn(1, 4)
    project(0, 1, t)
    siblings_rows(1)
    project(0, 1, other)
    rs_start(0, 1)
    w_shared(1)
    project(1, 0, t)
    project(1, 0, other)
    rs_start(1, 0)
    rs_finish(0, 0)
    project(1, 1, t)
    project(1, 1, other)
    rs_start(1, 1)
    rs_middle(0, 1)
    rs_middle(1, 0)
    rs_middle(1, 1)
    rs_finish(0, 1)
    pair(0, 0)
    rs_finish(1, 0)
    pair(0, 1)
    rs_finish(1, 1)
    pair(1, 0)
    paired(0)

    image = images[slot, x]
    scale = 1.0 / math.sqrt(HD)
    lane = lax.broadcasted_iota(jnp.int32, (192, 128), 1)
    spot = lax.broadcasted_iota(jnp.int32, (1, 1024), 1)
    key_row = spot // 64 % 4 * 128 + spot // 32 % 2 * 64 + spot // 256 % 2 * 32 + spot % 32
    key_row = key_row + (spot // 512 + slot) % 2 * 512
    valid = jnp.broadcast_to(key_row, (192, 1024)) < counts[z // 2, image]

    def score_head(head, stats):
        q = q_ref[:, pl.ds(pl.multiple_of(head * 128, 128), 128)]
        s = lax.dot_general(q, kb_ref[...], (((1,), (1,)), ((), ())), preferred_element_type=F32) * scale
        s = jnp.where(valid, s, -1e30)
        peak = jnp.max(s, axis=-1, keepdims=True)
        e = jnp.exp(s - peak)
        total = jnp.sum(e, axis=-1, keepdims=True)
        pr_ref[head] = e.astype(BF)
        return jnp.where(lane == head, peak, jnp.where(lane == head + 8, total, stats))

    stats = lax.fori_loop(0, 4, score_head, jnp.zeros((192, 128), F32))
    pair(1, 1)
    st_ref[...] = lax.fori_loop(4, 8, score_head, stats)

    def share_of(d):
        return pl.ds(pl.multiple_of(zm(d) // 2 * 48, 16), 48)

    for k, d in enumerate((2, 4, 6)):
        send(st_ref.at[share_of(d), :], zs_ref.at[k + 1], zs_send.at[k], zs_recv.at[k], to_z(d))
    zs_ref[0] = st_ref[share_of(0), :]

    paired(1)

    def weigh_head(head, carry):
        o = jnp.dot(pr_ref[head], vb_ref[...], preferred_element_type=F32)
        o_ref[:, pl.ds(pl.multiple_of(head * 128, 128), 128)] = o.astype(BF)
        return carry

    for half in range(2):
        lax.fori_loop(half * 4, half * 4 + 4, weigh_head, 0)
        for k, d in enumerate((2, 4, 6)):
            n = half * 3 + k
            part = o_ref.at[share_of(d), pl.ds(half * 512, 512)]
            send(part, zo_ref.at[half, k + 1], zo_send.at[n], zo_recv.at[n], to_z(d))
        zo_ref[half, 0] = o_ref[share_of(0), half * 512 : half * 512 + 512]
    for k in range(3):
        arrived(zs_ref.at[k + 1], zs_recv.at[k])
    stats = [zs_ref[k] for k in range(4)]
    peak = jnp.maximum(jnp.maximum(stats[0], stats[1]), jnp.maximum(stats[2], stats[3]))
    shares = [jnp.exp(s - peak) for s in stats]
    total = jnp.zeros((48, 128), F32)
    for k in range(4):
        total = total + shares[k] * pltpu.roll(stats[k], 120, 1)
    shares = [share / total for share in shares]

    def combine(half):
        for k in range(3):
            arrived(zo_ref.at[half, k + 1], zo_recv.at[half * 3 + k])
        for head in range(4):
            cols = pl.ds(head * 128, 128)
            h = half * 4 + head
            sums = jnp.zeros((48, 128), F32)
            for k in range(4):
                sums = sums + zo_ref[half, k, :, cols].astype(F32) * shares[k][:, h : h + 1]
            done = sums.astype(BF)
            if half == 0:
                at1[y, z, :, cols] = done
            else:
                at2[z, y, :, cols] = done

    def z1_step(s):
        for way, sign in ((0, -1), (1, 1)):
            if s < 4 or way == 0:
                block = at1.at[y, zm(sign * (s - 1))]
                send(block, block, z1_send.at[way, s - 1], z1_recv.at[way, s - 1], to_z(-sign))

    def z1_wait(s):
        for way, sign in ((0, -1), (1, 1)):
            if s < 4 or way == 0:
                arrived(at1.at[y, zm(sign * s)], z1_recv.at[way, s - 1])

    def z2_step(s, c):
        for way, sign in ((0, -1), (1, 1)):
            if s < 4 or way == c % 2:
                block = at2.at[zm(sign * (s - 1)), ym(-c)]
                k = (c * 2 + way) * 4 + s - 1
                send(block, block, z2_send.at[k], z2_recv.at[k], to_z(-sign))

    def z2_wait(s, c):
        for way, sign in ((0, -1), (1, 1)):
            if s < 4 or way == c % 2:
                k = (c * 2 + way) * 4 + s - 1
                arrived(at2.at[zm(sign * s), ym(-c)], z2_recv.at[k])

    def y1_step(offsets):
        for off in offsets:
            block = at1.at[y, zm(off)]
            for d in (2, 1, 3):
                k = (d - 1) * 8 + off + 3
                send(block, block, y1_send.at[k], y1_recv.at[k], to_y(d))

    combine(0)
    z1_step(1)
    y1_step((0,))
    combine(1)
    for d in (2, 1, 3):
        send(at2.at[z, y], at2.at[z, y], y2_send.at[d - 1], y2_recv.at[d - 1], to_y(d))
    z2_step(1, 0)
    for c in (1, 3, 2):
        arrived(at2.at[z, ym(-c)], y2_recv.at[c - 1])
        z2_step(1, c)
    for s in (1, 2, 3):
        z1_wait(s)
        z1_step(s + 1)
        y1_step((-s, s))
        for c in (0, 1, 3, 2):
            z2_wait(s, c)
            z2_step(s + 1, c)
    z1_wait(4)
    y1_step((4,))
    for c in (0, 1, 3, 2):
        z2_wait(4, c)

    acc = jnp.zeros((384, 256), F32)
    for block in range(NY):
        acc = acc + jnp.dot(
            at2[:, block].reshape(384, NARROW), ow_ref[block * 1024 + WIDE : block * 1024 + 1024],
            preferred_element_type=F32,
        )
    for d in (0, 1, 3, 2):
        if d > 0:
            for off in range(-3, 5):
                arrived(at1.at[ym(-d), zm(off)], y1_recv.at[(d - 1) * 8 + off + 3])
        rows = pl.ds(pl.multiple_of(ym(-d) * 1024, 1024), WIDE)
        acc = acc + jnp.dot(at1[ym(-d)].reshape(384, WIDE), ow_ref[rows], preferred_element_type=F32)
    acc_ref[...] = acc.reshape(4, 2, 48, 256)
    cs_ref[...] = acc_ref[:, other].reshape(192, 256).astype(BF)
    send(cs_ref, cr_ref, c_send, c_recv, sibling)
    mine_sum = acc_ref[:, t].reshape(192, 256)
    arrived(cr_ref, c_recv)
    out[...] = ((mine_sum + cr_ref[...].astype(F32)) * jnp.tanh(gate[...])).astype(BF)

    for copy in sends:
        copy.wait_send()
    for kind in range(2):
        for d in (1, 2, 3):
            arrived(w_ref.at[kind, :, third[0], :], wx_send.at[kind, d - 1])
            arrived(a_ref.at[kind, y, t], f_send.at[kind, d - 1])
    arrived(a_ref.at[:, y, t], c_fsend.at[6])


def local(features, kv_weights, key_gain, queries, out_weight, attn_gate, group_images, tile_valid):
    anywhere = pl.BlockSpec(memory_space=pl.ANY)
    vmem = pl.BlockSpec(memory_space=pltpu.VMEM)
    smem = pl.BlockSpec(memory_space=pltpu.SMEM)
    dma = pltpu.SemaphoreType.DMA
    return pl.pallas_call(
        fused,
        out_shape=jax.ShapeDtypeStruct((192, 256), BF),
        in_specs=[anywhere, anywhere, vmem, anywhere, anywhere, vmem, anywhere, anywhere],
        out_specs=vmem,
        scratch_shapes=[
            pltpu.SMEM((2, 4), jnp.int32),
            pltpu.SMEM((4, 8), jnp.int32),
            pltpu.VMEM((2, NY, 2, 2, 32, 2048), BF),
            pltpu.VMEM((2, NZ, 256, 512), BF),
            pltpu.VMEM((2, 2, 4, 2, 256, HD), BF),
            pltpu.VMEM((2, 2, 2, 256, HD), BF),
            pltpu.VMEM((2, 2, 2, 2, 256, HD), BF),
            pltpu.VMEM((4, 3, 256, HD), BF),
            pltpu.VMEM((NX, 256, HD), BF),
            pltpu.VMEM((NX, 256, HD), BF),
            pltpu.VMEM((NX, 256, HD), BF),
            pltpu.VMEM((NX, 256, HD), BF),
            pltpu.VMEM((4, 256, HD), BF),
            pltpu.VMEM((1024, HD), BF),
            pltpu.VMEM((1024, HD), BF),
            pltpu.VMEM((192, 1024), BF),
            pltpu.VMEM((8, 192, 1024), BF),
            pltpu.VMEM((192, 1024), BF),
            pltpu.VMEM((192, 128), F32),
            pltpu.VMEM((2, 4, 48, 512), BF),
            pltpu.VMEM((4, 48, 128), F32),
            pltpu.VMEM((NY, NZ, 48, WIDE), BF),
            pltpu.VMEM((NZ, NY, 48, NARROW), BF),
            pltpu.VMEM((4096, 256), BF),
            pltpu.VMEM((4, 2, 48, 256), F32),
            pltpu.VMEM((192, 256), BF),
            pltpu.VMEM((192, 256), BF),
            dma((9,)),
            dma((2, 3)), dma((2, 3)),
            dma((7,)), dma((7,)),
            dma((48,)), dma((48,)),
            dma((2, 3)), dma((2, 3)),
            dma((4, 6)), dma((4, 6)),
            dma((4, 3)), dma((4, 3)),
            dma((4,)), dma((4,)),
            dma((6,)), dma((6,)), dma((3,)), dma((3,)),
            dma((3,)), dma((3,)),
            dma((2, 4)), dma((2, 4)),
            dma((32,)), dma((32,)),
            dma((24,)), dma((24,)),
            dma, dma,
        ],
        compiler_params=pltpu.CompilerParams(
            collective_id=0, has_side_effects=True, vmem_limit_bytes=56 * 1024 * 1024
        ),
        name="fused",
    )(
        features, kv_weights, key_gain.reshape(1, HD), queries, out_weight,
        attn_gate.reshape(1, 1), group_images.T, tile_valid.T,
    )


def solution(mesh):
    placed = (
        P("group", ("img", "tensor"), None),
        P(None, "img", "tensor"),
        P(),
        P("group", "tensor"),
        P("tensor", "img"),
        P(),
        P(),
        P(),
    )
    return jax.shard_map(
        local, mesh=mesh, in_specs=placed, out_specs=P(("group", "tensor"), "img"), check_vma=False
    )
```

```python
import math

import jax
import jax.numpy as jnp
from jax import lax
from jax.experimental import pallas as pl
from jax.experimental.pallas import tpu as pltpu
from jax.sharding import PartitionSpec as P

HD = 128
MESH = pl.DeviceIdType.MESH
BF = jnp.bfloat16
F32 = jnp.float32
NX, NY, NZ = 4, 4, 8


def fused(
    feat, kvw, gain, queries, out_w, gate, images_hbm, counts_hbm, out,
    images, counts, a_ref, w_ref, p_ref, rs_relay, rs_recv, xs_ref, xk0_ref, xk1_ref, xv0_ref, xv1_ref, ps_ref, kb_ref, vb_ref,
    q_ref, pr_ref, o_ref, st_ref, zo_ref, zs_ref, at_ref, ow_ref, po_ref, fr_ref,
    loc_sem, f_send, f_recv, c_fsend, c_frecv, w_send, w_recv, wx_send, wx_recv,
    rs_send, rs_rsem, x_send, x_recv, pair_send, pair_recv, zo_send, zo_recv, zs_send, zs_recv,
    ow_send, ow_recv, g_send, g_recv, po_send, po_recv,
):
    x = lax.axis_index("group")
    img = lax.axis_index("img")
    t = lax.axis_index("tensor")
    z = img // NY
    y = img % NY
    other = 1 - t
    slot = z % 2

    def ym(d):
        return (y + d + NY) % NY

    def zm(d):
        return (z + d + NZ) % NZ

    def xm(d):
        return (x + d + NX) % NX

    def to_y(d):
        return {"img": z * NY + ym(d)}

    def to_z(d):
        return {"img": zm(d) * NY + y}

    def to_x(d):
        return {"group": xm(d)}

    sibling = {"tensor": other}
    partner = {"img": (z + 1 - 2 * slot) * NY + y}
    sends = []

    def remote(src, dst, ssem, rsem, where):
        return pltpu.make_async_remote_copy(
            src_ref=src, dst_ref=dst, send_sem=ssem, recv_sem=rsem,
            device_id=where, device_id_type=MESH,
        )

    def send(src, dst, ssem, rsem, where):
        copy = remote(src, dst, ssem, rsem, where)
        copy.start()
        sends.append(copy)

    def arrived(ref, sem):
        pltpu.make_async_copy(ref, ref, sem).wait()

    locals_ = []

    def fetch(src, dst, sem):
        copy = pltpu.make_async_copy(src, dst, sem)
        copy.start()
        locals_.append(copy)

    third = (
        pl.ds(pl.multiple_of(128 + x * 32, 32), 32),
        pl.ds(pl.multiple_of(128 + x * 32, 16), 16),
        pl.ds(pl.multiple_of(128 + x * 32 + 16, 16), 16),
    )

    def columns(block, kind):
        return pl.ds(pl.multiple_of((block * NY + kind) * 256, 256), 256)

    def place(block):
        return pl.ds(pl.multiple_of(block * 256, 256), 256)

    def fetch_own(block, carry):
        for half in range(2):
            own = feat.at[:, pl.ds(half * 32, 32), columns(block, y)]
            pltpu.make_async_copy(own, a_ref.at[half, y, t, :, :, place(block)], loc_sem.at[0]).start()
        return carry

    lax.fori_loop(0, NZ, fetch_own, 0)
    fetch(images_hbm, images, loc_sem.at[1])
    fetch(counts_hbm, counts, loc_sem.at[2])
    for kind in range(2):
        fetch(kvw.at[kind, pl.ds(0, 128), :], w_ref.at[kind, z, pl.ds(0, 128), :], loc_sem.at[3 + kind])
        fetch(kvw.at[kind, third[0], :], w_ref.at[kind, z, third[0], :], loc_sem.at[5 + kind])
    q_rows = pl.ds(pl.multiple_of(slot * 192, 64), 192)
    fetch(queries.at[q_rows, pl.ds(pl.multiple_of(y * 1024, 1024), 1024)], q_ref, loc_sem.at[7])
    mine = pl.ds(pl.multiple_of(y * 1024, 1024), 1024)
    fetch(out_w.at[mine, :], ow_ref.at[y], loc_sem.at[8])

    barrier = pltpu.get_barrier_semaphore()
    partners = [sibling] + [to_y(d) for d in (1, 2, 3)] + [to_x(d) for d in (1, 2, 3)]
    partners += [to_z(d) for d in (1, 2, 4, 6, 7)]
    partners += [{**to_y(d), **sibling} for d in (1, 2, 3)]
    for where in partners:
        pl.semaphore_signal(barrier, inc=1, device_id=where, device_id_type=MESH)
    pl.semaphore_wait(barrier, len(partners))

    def w_parts(s, way):
        if s < 4:
            return (third[0], pl.ds(0, 64), pl.ds(64, 64))
        return (third[1 + way], pl.ds(64 * way, 64))

    def w_start(kind, s, way, part):
        rows = w_parts(s, way)[part]
        sign = 2 * way - 1
        origin = zm(sign * (s - 1))
        src = kvw.at[kind, rows, :] if s == 1 else w_ref.at[kind, origin, rows, :]
        k = ((kind * 2 + way) * 4 + s - 1) * 3 + part
        send(src, w_ref.at[kind, origin, rows, :], w_send.at[k], w_recv.at[k], to_z(-sign))

    def w_begin(kind):
        for part in range(3):
            for way in range(2):
                w_start(kind, 1, way, part)
        w_share(kind, (0,))

    def w_turn(kind, s):
        for part in range(3):
            for way in range(2):
                rows = w_parts(s, way)
                if part < len(rows):
                    k = ((kind * 2 + way) * 4 + s - 1) * 3 + part
                    arrived(w_ref.at[kind, zm((2 * way - 1) * s), rows[part], :], w_recv.at[k])
                if s < 3 or (s == 3 and (part == 0 or part == 1 + way)):
                    w_start(kind, s + 1, way, min(part, 1) if s == 3 else part)
            if part == 0:
                w_share(kind, (-s, s) if s < 4 else (4,))

    def w_share(kind, offsets):
        for off in offsets:
            dst = w_ref.at[kind, zm(off), third[0], :]
            src = kvw.at[kind, third[0], :] if off == 0 else dst
            for d in (2, 1, 3):
                remote(src, dst, wx_send.at[kind, d - 1], wx_recv.at[kind, d - 1], to_x(d)).start()

    def w_shared(kind):
        for d in (1, 2, 3):
            rows = pl.ds(pl.multiple_of(128 + xm(-d) * 32, 32), 32)
            arrived(w_ref.at[kind, :, rows, :], wx_recv.at[kind, d - 1])

    def start_half(half):
        def start(block, carry):
            for d in (2, 1, 3):
                remote(
                    feat.at[:, pl.ds(half * 32, 32), columns(block, ym(d))],
                    a_ref.at[half, y, t, :, :, place(block)],
                    f_send.at[half, d - 1], f_recv.at[half, d - 1], to_y(d),
                ).start()
            return carry

        lax.fori_loop(0, NZ, start, 0)

    def start_own(block, carry):
        for half in range(2):
            own = feat.at[:, pl.ds(half * 32, 32), columns(block, y)]
            remote(own, a_ref.at[half, y, t, :, :, place(block)], c_fsend.at[6], c_frecv.at[6], sibling).start()
        return carry

    def pass_half(half):
        for d in (1, 2, 3):
            block = a_ref.at[half, ym(-d), t]
            arrived(block, f_recv.at[half, d - 1])
            k = half * 3 + d - 1
            send(block, block, c_fsend.at[k], c_frecv.at[k], sibling)

    def project(kind, half, core):
        rows = a_ref[half, :, core].reshape(256, 2048)
        part = jnp.dot(rows, w_ref[kind].reshape(2048, 512), preferred_element_type=F32).astype(BF)
        for src in range(4):
            for image in range(2):
                first = src * 64 + image * 32
                where = pl.ds(pl.multiple_of(src * 64 + core * 32, 32), 32)
                for head in range(4):
                    p_ref[kind, half, head, image, where, :] = part[first : first + 32, head * 128 : head * 128 + 128]

    def siblings_rows(half):
        if half == 0:
            arrived(a_ref.at[:, y, other], c_frecv.at[6])
        for d in (1, 2, 3):
            arrived(a_ref.at[half, ym(-d), other], c_frecv.at[half * 3 + d - 1])

    def rs_start(kind, half):
        p, ss, rr = p_ref.at[kind, half], rs_send.at[kind * 2 + half], rs_rsem.at[kind * 2 + half]
        got, via = rs_recv.at[kind, half], rs_relay.at[kind, half]
        send(p.at[ym(2), 0], via.at[0], ss.at[0], rr.at[0], to_y(1))
        send(p.at[ym(2), 1], via.at[1], ss.at[1], rr.at[1], to_y(-1))
        send(p.at[ym(1), 1], got.at[0, 1], ss.at[2], rr.at[2], to_y(1))
        send(p.at[ym(-1), 0], got.at[1, 0], ss.at[3], rr.at[3], to_y(-1))

    def rs_middle(kind, half):
        p, ss, rr = p_ref.at[kind, half], rs_send.at[kind * 2 + half], rs_rsem.at[kind * 2 + half]
        got, via = rs_recv.at[kind, half], rs_relay.at[kind, half]
        for way, d in ((0, 1), (1, -1)):
            arrived(via.at[way], rr.at[way])
            p[ym(d), way] = (p[ym(d), way].astype(F32) + via[way].astype(F32)).astype(BF)
            send(p.at[ym(d), way], got.at[way, way], ss.at[4 + way], rr.at[4 + way], to_y(d))

    x_refs = (xk0_ref, xk1_ref, xv0_ref, xv1_ref)

    def rs_finish(kind, half):
        n = kind * 2 + half
        p, rr, got, xr_ref = p_ref.at[kind, half], rs_rsem.at[n], rs_recv.at[kind, half], x_refs[n]
        arrived(got.at[0, 1], rr.at[2])
        arrived(got.at[1, 0], rr.at[3])
        arrived(got.at[0, 0], rr.at[4])
        arrived(got.at[1, 1], rr.at[5])
        both = []
        for image in range(2):
            total = p[y, image].astype(F32) + got[0, image].astype(F32) + got[1, image].astype(F32)
            if kind == 0:
                mean = jnp.mean(total * total, axis=-1, keepdims=True)
                total = total * lax.rsqrt(mean + 1e-05) * gain[...]
            both.append(total.astype(BF))
        for d in (2, 1, 3, 0):
            group = xm(d)
            second = (images[0, group] == 2 * x + 1) | (images[1, group] == 2 * x + 1)
            block = jnp.where(second, both[1], both[0])
            if d == 0:
                xr_ref[x] = block
            else:
                xs_ref[n, d - 1] = block
                send(xs_ref.at[n, d - 1], xr_ref.at[x], x_send.at[n, d - 1], x_recv.at[n, d - 1], to_x(d))

    def pair(kind, half):
        n = kind * 2 + half
        xr_ref, both_ref = x_refs[n], (kb_ref, vb_ref)[kind]
        for d in range(1, NX):
            arrived(xr_ref.at[xm(-d)], x_recv.at[n, d - 1])
        ps_ref[n] = xr_ref[images[1 - slot, x] // 2]
        send(ps_ref.at[n], both_ref.at[pl.ds(512 + half * 256, 256)], pair_send.at[n], pair_recv.at[n], partner)
        both_ref[half * 256 : half * 256 + 256] = xr_ref[images[slot, x] // 2]

    def paired(kind):
        both_ref = (kb_ref, vb_ref)[kind]
        for half in range(2):
            arrived(both_ref.at[pl.ds(512 + half * 256, 256)], pair_recv.at[kind * 2 + half])

    w_begin(0)
    start_half(0)
    start_half(1)
    lax.fori_loop(0, NZ, start_own, 0)
    w_turn(0, 1)
    w_begin(1)
    w_turn(0, 2)
    w_turn(1, 1)
    pass_half(0)
    w_turn(0, 3)
    w_turn(1, 2)
    w_turn(0, 4)
    arrived(a_ref.at[:, y, t], loc_sem.at[0])
    for copy in locals_:
        copy.wait()
    w_shared(0)
    project(0, 0, t)
    siblings_rows(0)
    project(0, 0, other)
    rs_start(0, 0)
    w_turn(1, 3)
    pass_half(1)
    rs_middle(0, 0)
    w_turn(1, 4)
    project(0, 1, t)
    siblings_rows(1)
    project(0, 1, other)
    rs_start(0, 1)
    w_shared(1)
    project(1, 0, t)
    project(1, 0, other)
    rs_start(1, 0)
    rs_finish(0, 0)
    project(1, 1, t)
    project(1, 1, other)
    rs_start(1, 1)
    rs_middle(0, 1)
    rs_middle(1, 0)
    rs_middle(1, 1)
    for d in (2, 1, 3):
        rows = pl.ds(pl.multiple_of(ym(d) * 1024, 1024), 1024)
        send(out_w.at[rows, :], ow_ref.at[y], ow_send.at[d - 1], ow_recv.at[d - 1], to_y(d))
    rs_finish(0, 1)
    pair(0, 0)
    rs_finish(1, 0)
    pair(0, 1)
    rs_finish(1, 1)
    pair(1, 0)
    paired(0)

    image = images[slot, x]
    scale = 1.0 / math.sqrt(HD)
    lane = lax.broadcasted_iota(jnp.int32, (192, 128), 1)
    spot = lax.broadcasted_iota(jnp.int32, (1, 1024), 1)
    key_row = spot // 64 % 4 * 128 + spot // 32 % 2 * 64 + spot // 256 % 2 * 32 + spot % 32
    key_row = key_row + (spot // 512 + slot) % 2 * 512
    valid = jnp.broadcast_to(key_row, (192, 1024)) < counts[z // 2, image]

    def score_head(head, stats):
        q = q_ref[:, pl.ds(pl.multiple_of(head * 128, 128), 128)]
        s = lax.dot_general(q, kb_ref[...], (((1,), (1,)), ((), ())), preferred_element_type=F32) * scale
        s = jnp.where(valid, s, -1e30)
        peak = jnp.max(s, axis=-1, keepdims=True)
        e = jnp.exp(s - peak)
        total = jnp.sum(e, axis=-1, keepdims=True)
        pr_ref[head] = e.astype(BF)
        return jnp.where(lane == head, peak, jnp.where(lane == head + 8, total, stats))

    stats = lax.fori_loop(0, 4, score_head, jnp.zeros((192, 128), F32))
    pair(1, 1)
    st_ref[...] = lax.fori_loop(4, 8, score_head, stats)

    def share_of(d):
        return pl.ds(pl.multiple_of(zm(d) // 2 * 48, 16), 48)

    for k, d in enumerate((2, 4, 6)):
        send(st_ref.at[share_of(d), :], zs_ref.at[k + 1], zs_send.at[k], zs_recv.at[k], to_z(d))
    zs_ref[0] = st_ref[share_of(0), :]

    paired(1)

    def weigh_head(head, carry):
        o = jnp.dot(pr_ref[head], vb_ref[...], preferred_element_type=F32)
        o_ref[:, pl.ds(pl.multiple_of(head * 128, 128), 128)] = o.astype(BF)
        return carry

    for half in range(2):
        lax.fori_loop(half * 4, half * 4 + 4, weigh_head, 0)
        for k, d in enumerate((2, 4, 6)):
            n = half * 3 + k
            part = o_ref.at[share_of(d), pl.ds(half * 512, 512)]
            send(part, zo_ref.at[half, k + 1], zo_send.at[n], zo_recv.at[n], to_z(d))
        zo_ref[half, 0] = o_ref[share_of(0), half * 512 : half * 512 + 512]
    for k in range(3):
        arrived(zs_ref.at[k + 1], zs_recv.at[k])
    stats = [zs_ref[k] for k in range(4)]
    peak = jnp.maximum(jnp.maximum(stats[0], stats[1]), jnp.maximum(stats[2], stats[3]))
    shares = [jnp.exp(s - peak) for s in stats]
    total = jnp.zeros((48, 128), F32)
    for k in range(4):
        total = total + shares[k] * pltpu.roll(stats[k], 120, 1)
    shares = [share / total for share in shares]

    def combine(half):
        for k in range(3):
            arrived(zo_ref.at[half, k + 1], zo_recv.at[half * 3 + k])
        for head in range(4):
            cols = pl.ds(head * 128, 128)
            h = half * 4 + head
            sums = jnp.zeros((48, 128), F32)
            for k in range(4):
                sums = sums + zo_ref[half, k, :, cols].astype(F32) * shares[k][:, h : h + 1]
            done = sums.astype(BF)
            at_ref[half, z, :, cols] = done

    def gather_near(half):
        block = at_ref.at[half, z]
        for d in (2, 6, 1, 7):
            send(block, block, g_send.at[half, d], g_recv.at[half, d], to_z(d))

    def gather_far(half):
        for d in (2, 6, 1, 7):
            arrived(at_ref.at[half, zm(-d)], g_recv.at[half, d])
        across = 2 if half == 0 else 6
        block = at_ref.at[half, zm(-across)]
        send(block, block, g_send.at[half, 4], g_recv.at[half, 4], to_z(across))
        for d in (1, 7):
            block = at_ref.at[half, zm(-2 if d == 1 else 2)]
            k = 3 if d == 1 else 5
            send(block, block, g_send.at[half, k], g_recv.at[half, k], to_z(d))

    def gathered(half):
        for k in (4, 3, 5):
            arrived(at_ref.at[half, zm(-k)], g_recv.at[half, k])

    keep = (z + t) % 2

    def project_out(group):
        offsets = (0, 2, -1, 1) if group == 0 else (-2, 4, -3, 3)
        rows = [
            jnp.concatenate([at_ref[half, zm(off)] for off in offsets], axis=0) for half in range(2)
        ]
        for d in (2, 1, 3, 0):
            part = jnp.dot(rows[0], ow_ref[ym(d), 0:512], preferred_element_type=F32)
            part = part + jnp.dot(rows[1], ow_ref[ym(d), 512:1024], preferred_element_type=F32)
            part = part.astype(BF)
            po_ref[group, d, 0] = part[0:96]
            po_ref[group, d, 1] = part[96:192]
            for core in range(2):
                block = po_ref.at[group, d, (keep + core) % 2]
                k = (group * 4 + d) * 2 + core
                if d > 0:
                    where = to_y(d) if core == 0 else {**to_y(d), **sibling}
                    send(block, fr_ref.at[group, d, core], po_send.at[k], po_recv.at[k], where)
                elif core == 1:
                    send(block, fr_ref.at[group, d, core], po_send.at[k], po_recv.at[k], sibling)

    def finish_out(group):
        total = po_ref[group, 0, keep].astype(F32)
        for d in range(4):
            for core in range(2):
                if d > 0 or core == 1:
                    arrived(fr_ref.at[group, d, core], po_recv.at[(group * 4 + d) * 2 + core])
                    total = total + fr_ref[group, d, core].astype(F32)
        total = (total * jnp.tanh(gate[...])).astype(BF)
        for i in range(2):
            off = 2 * i - keep if group == 0 else 6 * i - 2 - keep
            rows = pl.ds(pl.multiple_of(zm(off) // 2 * 48, 16), 48)
            out[rows, :] = total[i * 48 : i * 48 + 48]

    combine(0)
    gather_near(0)
    combine(1)
    gather_near(1)
    gather_far(0)
    gather_far(1)
    for d in (1, 2, 3):
        arrived(ow_ref.at[ym(-d)], ow_recv.at[d - 1])
    project_out(0)
    gathered(0)
    gathered(1)
    project_out(1)
    finish_out(0)
    finish_out(1)

    for copy in sends:
        copy.wait_send()
    for kind in range(2):
        for d in (1, 2, 3):
            arrived(w_ref.at[kind, :, third[0], :], wx_send.at[kind, d - 1])
            arrived(a_ref.at[kind, y, t], f_send.at[kind, d - 1])
    arrived(a_ref.at[:, y, t], c_fsend.at[6])


def local(features, kv_weights, key_gain, queries, out_weight, attn_gate, group_images, tile_valid):
    anywhere = pl.BlockSpec(memory_space=pl.ANY)
    vmem = pl.BlockSpec(memory_space=pltpu.VMEM)
    smem = pl.BlockSpec(memory_space=pltpu.SMEM)
    dma = pltpu.SemaphoreType.DMA
    return pl.pallas_call(
        fused,
        out_shape=jax.ShapeDtypeStruct((192, 256), BF),
        in_specs=[anywhere, anywhere, vmem, anywhere, anywhere, vmem, anywhere, anywhere],
        out_specs=vmem,
        scratch_shapes=[
            pltpu.SMEM((2, 4), jnp.int32),
            pltpu.SMEM((4, 8), jnp.int32),
            pltpu.VMEM((2, NY, 2, 2, 32, 2048), BF),
            pltpu.VMEM((2, NZ, 256, 512), BF),
            pltpu.VMEM((2, 2, 4, 2, 256, HD), BF),
            pltpu.VMEM((2, 2, 2, 256, HD), BF),
            pltpu.VMEM((2, 2, 2, 2, 256, HD), BF),
            pltpu.VMEM((4, 3, 256, HD), BF),
            pltpu.VMEM((NX, 256, HD), BF),
            pltpu.VMEM((NX, 256, HD), BF),
            pltpu.VMEM((NX, 256, HD), BF),
            pltpu.VMEM((NX, 256, HD), BF),
            pltpu.VMEM((4, 256, HD), BF),
            pltpu.VMEM((1024, HD), BF),
            pltpu.VMEM((1024, HD), BF),
            pltpu.VMEM((192, 1024), BF),
            pltpu.VMEM((8, 192, 1024), BF),
            pltpu.VMEM((192, 1024), BF),
            pltpu.VMEM((192, 128), F32),
            pltpu.VMEM((2, 4, 48, 512), BF),
            pltpu.VMEM((4, 48, 128), F32),
            pltpu.VMEM((2, NZ, 48, 512), BF),
            pltpu.VMEM((NY, 1024, 256), BF),
            pltpu.VMEM((2, 4, 2, 96, 256), BF),
            pltpu.VMEM((2, 4, 2, 96, 256), BF),
            dma((9,)),
            dma((2, 3)), dma((2, 3)),
            dma((7,)), dma((7,)),
            dma((48,)), dma((48,)),
            dma((2, 3)), dma((2, 3)),
            dma((4, 6)), dma((4, 6)),
            dma((4, 3)), dma((4, 3)),
            dma((4,)), dma((4,)),
            dma((6,)), dma((6,)), dma((3,)), dma((3,)),
            dma((3,)), dma((3,)),
            dma((2, 8)), dma((2, 8)),
            dma((16,)), dma((16,)),
        ],
        compiler_params=pltpu.CompilerParams(
            collective_id=0, has_side_effects=True, vmem_limit_bytes=56 * 1024 * 1024
        ),
        name="fused",
    )(
        features, kv_weights, key_gain.reshape(1, HD), queries, out_weight,
        attn_gate.reshape(1, 1), group_images.T, tile_valid.T,
    )


def solution(mesh):
    placed = (
        P("group", ("img", "tensor"), None),
        P(None, "img", "tensor"),
        P(),
        P("group", "tensor"),
        P("tensor", "img"),
        P(),
        P(),
        P(),
    )
    return jax.shard_map(
        local, mesh=mesh, in_specs=placed, out_specs=P(("group", "tensor"), "img"), check_vma=False
    )
```

```python
import math

import jax
import jax.numpy as jnp
from jax import lax
from jax.experimental import pallas as pl
from jax.experimental.pallas import tpu as pltpu
from jax.sharding import PartitionSpec as P

HD = 128
MESH = pl.DeviceIdType.MESH
BF = jnp.bfloat16
F32 = jnp.float32
NX, NY, NZ = 4, 4, 8


def fused(
    feat, kvw, gain, queries, out_w, gate, images_hbm, counts_hbm, out,
    images, counts, a_ref, w_ref, p_ref, rs_relay, rs_recv, xs_ref, xk0_ref, xk1_ref, xv0_ref, xv1_ref, ps_ref, kb_ref, vb_ref,
    q_ref, pr_ref, o_ref, st_ref, zo_ref, zs_ref, at_ref, ow_ref, po_ref, fr_ref,
    loc_sem, f_send, f_recv, c_fsend, c_frecv, w_send, w_recv, wx_send, wx_recv,
    rs_send, rs_rsem, x_send, x_recv, pair_send, pair_recv, zo_send, zo_recv, zs_send, zs_recv,
    ow_send, ow_recv, g_send, g_recv, po_send, po_recv,
):
    x = lax.axis_index("group")
    img = lax.axis_index("img")
    t = lax.axis_index("tensor")
    z = img // NY
    y = img % NY
    other = 1 - t
    slot = z % 2

    def ym(d):
        return (y + d + NY) % NY

    def zm(d):
        return (z + d + NZ) % NZ

    def xm(d):
        return (x + d + NX) % NX

    def to_y(d):
        return {"img": z * NY + ym(d)}

    def to_z(d):
        return {"img": zm(d) * NY + y}

    def to_x(d):
        return {"group": xm(d)}

    sibling = {"tensor": other}
    partner = {"img": (z + 1 - 2 * slot) * NY + y}
    sends = []

    def remote(src, dst, ssem, rsem, where):
        return pltpu.make_async_remote_copy(
            src_ref=src, dst_ref=dst, send_sem=ssem, recv_sem=rsem,
            device_id=where, device_id_type=MESH,
        )

    def send(src, dst, ssem, rsem, where):
        copy = remote(src, dst, ssem, rsem, where)
        copy.start()
        sends.append(copy)

    def arrived(ref, sem):
        pltpu.make_async_copy(ref, ref, sem).wait()

    locals_ = []

    def fetch(src, dst, sem):
        copy = pltpu.make_async_copy(src, dst, sem)
        copy.start()
        locals_.append(copy)

    third = (
        pl.ds(pl.multiple_of(128 + x * 32, 32), 32),
        pl.ds(pl.multiple_of(128 + x * 32, 16), 16),
        pl.ds(pl.multiple_of(128 + x * 32 + 16, 16), 16),
    )

    def columns(block, kind):
        return pl.ds(pl.multiple_of((block * NY + kind) * 256, 256), 256)

    def place(block):
        return pl.ds(pl.multiple_of(block * 256, 256), 256)

    def fetch_own(block, carry):
        for half in range(2):
            own = feat.at[:, pl.ds(half * 32, 32), columns(block, y)]
            pltpu.make_async_copy(own, a_ref.at[half, y, t, :, :, place(block)], loc_sem.at[0]).start()
        return carry

    lax.fori_loop(0, NZ, fetch_own, 0)
    fetch(images_hbm, images, loc_sem.at[1])
    fetch(counts_hbm, counts, loc_sem.at[2])
    for kind in range(2):
        fetch(kvw.at[kind, pl.ds(0, 128), :], w_ref.at[kind, z, pl.ds(0, 128), :], loc_sem.at[3 + kind])
        fetch(kvw.at[kind, third[0], :], w_ref.at[kind, z, third[0], :], loc_sem.at[5 + kind])
    q_rows = pl.ds(pl.multiple_of(slot * 192, 64), 192)
    fetch(queries.at[q_rows, pl.ds(pl.multiple_of(y * 1024, 1024), 1024)], q_ref, loc_sem.at[7])
    mine = pl.ds(pl.multiple_of(y * 1024, 1024), 1024)
    fetch(out_w.at[mine, :], ow_ref.at[y], loc_sem.at[8])

    barrier = pltpu.get_barrier_semaphore()
    partners = [sibling] + [to_y(d) for d in (1, 2, 3)] + [to_x(d) for d in (1, 2, 3)]
    partners += [to_z(d) for d in (1, 2, 4, 6, 7)]
    partners += [{**to_y(d), **sibling} for d in (1, 2, 3)]
    for where in partners:
        pl.semaphore_signal(barrier, inc=1, device_id=where, device_id_type=MESH)
    pl.semaphore_wait(barrier, len(partners))

    def w_parts(s, way):
        if s < 4:
            return (third[0], pl.ds(0, 64), pl.ds(64, 64))
        return (third[1 + way], pl.ds(64 * way, 64))

    def w_start(kind, s, way, part):
        rows = w_parts(s, way)[part]
        sign = 2 * way - 1
        origin = zm(sign * (s - 1))
        src = kvw.at[kind, rows, :] if s == 1 else w_ref.at[kind, origin, rows, :]
        k = ((kind * 2 + way) * 4 + s - 1) * 3 + part
        send(src, w_ref.at[kind, origin, rows, :], w_send.at[k], w_recv.at[k], to_z(-sign))

    def w_begin(kind):
        for part in range(3):
            for way in range(2):
                w_start(kind, 1, way, part)
        w_share(kind, (0,))

    def w_turn(kind, s):
        for part in range(3):
            for way in range(2):
                rows = w_parts(s, way)
                if part < len(rows):
                    k = ((kind * 2 + way) * 4 + s - 1) * 3 + part
                    arrived(w_ref.at[kind, zm((2 * way - 1) * s), rows[part], :], w_recv.at[k])
                if s < 3 or (s == 3 and (part == 0 or part == 1 + way)):
                    w_start(kind, s + 1, way, min(part, 1) if s == 3 else part)
            if part == 0:
                w_share(kind, (-s, s) if s < 4 else (4,))

    def w_share(kind, offsets):
        for off in offsets:
            dst = w_ref.at[kind, zm(off), third[0], :]
            src = kvw.at[kind, third[0], :] if off == 0 else dst
            for d in (2, 1, 3):
                remote(src, dst, wx_send.at[kind, d - 1], wx_recv.at[kind, d - 1], to_x(d)).start()

    def w_shared(kind):
        for d in (1, 2, 3):
            rows = pl.ds(pl.multiple_of(128 + xm(-d) * 32, 32), 32)
            arrived(w_ref.at[kind, :, rows, :], wx_recv.at[kind, d - 1])

    def start_half(half):
        def start(block, carry):
            for d in (2, 1, 3):
                remote(
                    feat.at[:, pl.ds(half * 32, 32), columns(block, ym(d))],
                    a_ref.at[half, y, t, :, :, place(block)],
                    f_send.at[half, d - 1], f_recv.at[half, d - 1], to_y(d),
                ).start()
            return carry

        lax.fori_loop(0, NZ, start, 0)

    def start_own(block, carry):
        for half in range(2):
            own = feat.at[:, pl.ds(half * 32, 32), columns(block, y)]
            remote(own, a_ref.at[half, y, t, :, :, place(block)], c_fsend.at[6], c_frecv.at[6], sibling).start()
        return carry

    def pass_half(half):
        for d in (1, 2, 3):
            block = a_ref.at[half, ym(-d), t]
            arrived(block, f_recv.at[half, d - 1])
            k = half * 3 + d - 1
            send(block, block, c_fsend.at[k], c_frecv.at[k], sibling)

    def project(kind, half, core):
        rows = (a_ref[half] if core is None else a_ref[half, :, core]).reshape(-1, 2048)
        part = jnp.dot(rows, w_ref[kind].reshape(2048, 512), preferred_element_type=F32).astype(BF)
        for src in range(4):
            for image in range(2):
                if core is None:
                    both = [part[src * 128 + c * 64 + image * 32 : src * 128 + c * 64 + image * 32 + 32] for c in range(2)]
                    rows = jnp.concatenate(both, axis=0)
                    where = pl.ds(src * 64, 64)
                else:
                    rows = part[src * 64 + image * 32 : src * 64 + image * 32 + 32]
                    where = pl.ds(pl.multiple_of(src * 64 + core * 32, 32), 32)
                for head in range(4):
                    p_ref[kind, half, head, image, where, :] = rows[:, head * 128 : head * 128 + 128]

    def siblings_rows(half):
        if half == 0:
            arrived(a_ref.at[:, y, other], c_frecv.at[6])
        for d in (1, 2, 3):
            arrived(a_ref.at[half, ym(-d), other], c_frecv.at[half * 3 + d - 1])

    def rs_start(kind, half):
        p, ss, rr = p_ref.at[kind, half], rs_send.at[kind * 2 + half], rs_rsem.at[kind * 2 + half]
        got, via = rs_recv.at[kind, half], rs_relay.at[kind, half]
        send(p.at[ym(2), 0], via.at[0], ss.at[0], rr.at[0], to_y(1))
        send(p.at[ym(2), 1], via.at[1], ss.at[1], rr.at[1], to_y(-1))
        send(p.at[ym(1), 1], got.at[0, 1], ss.at[2], rr.at[2], to_y(1))
        send(p.at[ym(-1), 0], got.at[1, 0], ss.at[3], rr.at[3], to_y(-1))

    def rs_middle(kind, half):
        p, ss, rr = p_ref.at[kind, half], rs_send.at[kind * 2 + half], rs_rsem.at[kind * 2 + half]
        got, via = rs_recv.at[kind, half], rs_relay.at[kind, half]
        for way, d in ((0, 1), (1, -1)):
            arrived(via.at[way], rr.at[way])
            p[ym(d), way] = (p[ym(d), way].astype(F32) + via[way].astype(F32)).astype(BF)
            send(p.at[ym(d), way], got.at[way, way], ss.at[4 + way], rr.at[4 + way], to_y(d))

    x_refs = (xk0_ref, xk1_ref, xv0_ref, xv1_ref)

    def rs_finish(kind, half):
        n = kind * 2 + half
        p, rr, got, xr_ref = p_ref.at[kind, half], rs_rsem.at[n], rs_recv.at[kind, half], x_refs[n]
        arrived(got.at[0, 1], rr.at[2])
        arrived(got.at[1, 0], rr.at[3])
        arrived(got.at[0, 0], rr.at[4])
        arrived(got.at[1, 1], rr.at[5])
        both = []
        for image in range(2):
            total = p[y, image].astype(F32) + got[0, image].astype(F32) + got[1, image].astype(F32)
            if kind == 0:
                mean = jnp.mean(total * total, axis=-1, keepdims=True)
                total = total * lax.rsqrt(mean + 1e-05) * gain[...]
            both.append(total.astype(BF))
        for d in (2, 1, 3, 0):
            group = xm(d)
            second = (images[0, group] == 2 * x + 1) | (images[1, group] == 2 * x + 1)
            block = jnp.where(second, both[1], both[0])
            if d == 0:
                xr_ref[x] = block
            else:
                xs_ref[n, d - 1] = block
                send(xs_ref.at[n, d - 1], xr_ref.at[x], x_send.at[n, d - 1], x_recv.at[n, d - 1], to_x(d))

    def pair(kind, half):
        n = kind * 2 + half
        xr_ref, both_ref = x_refs[n], (kb_ref, vb_ref)[kind]
        for d in range(1, NX):
            arrived(xr_ref.at[xm(-d)], x_recv.at[n, d - 1])
        ps_ref[n] = xr_ref[images[1 - slot, x] // 2]
        send(ps_ref.at[n], both_ref.at[pl.ds(512 + half * 256, 256)], pair_send.at[n], pair_recv.at[n], partner)
        both_ref[half * 256 : half * 256 + 256] = xr_ref[images[slot, x] // 2]

    def paired(kind):
        both_ref = (kb_ref, vb_ref)[kind]
        for half in range(2):
            arrived(both_ref.at[pl.ds(512 + half * 256, 256)], pair_recv.at[kind * 2 + half])

    w_begin(0)
    start_half(0)
    start_half(1)
    lax.fori_loop(0, NZ, start_own, 0)
    w_turn(0, 1)
    w_begin(1)
    w_turn(0, 2)
    w_turn(1, 1)
    pass_half(0)
    w_turn(0, 3)
    w_turn(1, 2)
    w_turn(0, 4)
    arrived(a_ref.at[:, y, t], loc_sem.at[0])
    for copy in locals_:
        copy.wait()
    w_shared(0)
    project(0, 0, t)
    siblings_rows(0)
    project(0, 0, other)
    rs_start(0, 0)
    w_turn(1, 3)
    pass_half(1)
    rs_middle(0, 0)
    w_turn(1, 4)
    project(0, 1, t)
    siblings_rows(1)
    project(0, 1, other)
    rs_start(0, 1)
    w_shared(1)
    project(1, 0, None)
    rs_start(1, 0)
    rs_finish(0, 0)
    project(1, 1, None)
    rs_start(1, 1)
    rs_middle(0, 1)
    rs_middle(1, 0)
    rs_middle(1, 1)
    rs_finish(0, 1)
    pair(0, 0)
    rs_finish(1, 0)
    pair(0, 1)
    rs_finish(1, 1)
    for d in (2, 1, 3):
        rows = pl.ds(pl.multiple_of(ym(d) * 1024, 1024), 1024)
        send(out_w.at[rows, :], ow_ref.at[y], ow_send.at[d - 1], ow_recv.at[d - 1], to_y(d))
    pair(1, 0)
    paired(0)

    image = images[slot, x]
    scale = 1.0 / math.sqrt(HD)
    lane = lax.broadcasted_iota(jnp.int32, (192, 128), 1)
    spot = lax.broadcasted_iota(jnp.int32, (1, 1024), 1)
    key_row = spot // 64 % 4 * 128 + spot // 32 % 2 * 64 + spot // 256 % 2 * 32 + spot % 32
    key_row = key_row + (spot // 512 + slot) % 2 * 512
    valid = jnp.broadcast_to(key_row, (192, 1024)) < counts[z // 2, image]

    def score_head(head, stats):
        q = q_ref[:, pl.ds(pl.multiple_of(head * 128, 128), 128)]
        s = lax.dot_general(q, kb_ref[...], (((1,), (1,)), ((), ())), preferred_element_type=F32) * scale
        s = jnp.where(valid, s, -1e30)
        peak = jnp.max(s, axis=-1, keepdims=True)
        e = jnp.exp(s - peak)
        total = jnp.sum(e, axis=-1, keepdims=True)
        pr_ref[head] = e.astype(BF)
        return jnp.where(lane == head, peak, jnp.where(lane == head + 8, total, stats))

    stats = lax.fori_loop(0, 4, score_head, jnp.zeros((192, 128), F32))
    pair(1, 1)
    st_ref[...] = lax.fori_loop(4, 8, score_head, stats)

    def share_of(d):
        return pl.ds(pl.multiple_of(zm(d) // 2 * 48, 16), 48)

    for k, d in enumerate((2, 4, 6)):
        send(st_ref.at[share_of(d), :], zs_ref.at[k + 1], zs_send.at[k], zs_recv.at[k], to_z(d))
    zs_ref[0] = st_ref[share_of(0), :]

    paired(1)

    def weigh_head(head, carry):
        o = jnp.dot(pr_ref[head], vb_ref[...], preferred_element_type=F32)
        o_ref[:, pl.ds(pl.multiple_of(head * 128, 128), 128)] = o.astype(BF)
        return carry

    for half in range(2):
        lax.fori_loop(half * 4, half * 4 + 4, weigh_head, 0)
        for k, d in enumerate((2, 4, 6)):
            n = half * 3 + k
            part = o_ref.at[share_of(d), pl.ds(half * 512, 512)]
            send(part, zo_ref.at[half, k + 1], zo_send.at[n], zo_recv.at[n], to_z(d))
        zo_ref[half, 0] = o_ref[share_of(0), half * 512 : half * 512 + 512]
    for k in range(3):
        arrived(zs_ref.at[k + 1], zs_recv.at[k])
    stats = [zs_ref[k] for k in range(4)]
    peak = jnp.maximum(jnp.maximum(stats[0], stats[1]), jnp.maximum(stats[2], stats[3]))
    shares = [jnp.exp(s - peak) for s in stats]
    total = jnp.zeros((48, 128), F32)
    for k in range(4):
        total = total + shares[k] * pltpu.roll(stats[k], 120, 1)
    shares = [share / total for share in shares]

    def combine(half):
        for k in range(3):
            arrived(zo_ref.at[half, k + 1], zo_recv.at[half * 3 + k])
        for head in range(4):
            cols = pl.ds(head * 128, 128)
            h = half * 4 + head
            sums = jnp.zeros((48, 128), F32)
            for k in range(4):
                sums = sums + zo_ref[half, k, :, cols].astype(F32) * shares[k][:, h : h + 1]
            done = sums.astype(BF)
            at_ref[half, z, :, cols] = done

    def gather_near(half):
        block = at_ref.at[half, z]
        for d in (2, 6, 1, 7):
            send(block, block, g_send.at[half, d], g_recv.at[half, d], to_z(d))

    def gather_far(half):
        for d in (2, 6, 1, 7):
            arrived(at_ref.at[half, zm(-d)], g_recv.at[half, d])
        across = 2 if half == 0 else 6
        block = at_ref.at[half, zm(-across)]
        send(block, block, g_send.at[half, 4], g_recv.at[half, 4], to_z(across))
        for d in (1, 7):
            block = at_ref.at[half, zm(-2 if d == 1 else 2)]
            k = 3 if d == 1 else 5
            send(block, block, g_send.at[half, k], g_recv.at[half, k], to_z(d))

    def gathered(half):
        for k in (4, 3, 5):
            arrived(at_ref.at[half, zm(-k)], g_recv.at[half, k])

    keep = (z + t) % 2

    def project_out(group):
        offsets = (0, 2, -1, 1) if group == 0 else (-2, 4, -3, 3)
        rows = [
            jnp.concatenate([at_ref[half, zm(off)] for off in offsets], axis=0) for half in range(2)
        ]
        for d in (2, 1, 3, 0):
            part = jnp.dot(rows[0], ow_ref[ym(d), 0:512], preferred_element_type=F32)
            part = part + jnp.dot(rows[1], ow_ref[ym(d), 512:1024], preferred_element_type=F32)
            part = part.astype(BF)
            po_ref[group, d, 0] = part[0:96]
            po_ref[group, d, 1] = part[96:192]
            for core in range(2):
                block = po_ref.at[group, d, (keep + core) % 2]
                k = (group * 4 + d) * 2 + core
                if d > 0:
                    where = to_y(d) if core == 0 else {**to_y(d), **sibling}
                    send(block, fr_ref.at[group, d, core], po_send.at[k], po_recv.at[k], where)
                elif core == 1:
                    send(block, fr_ref.at[group, d, core], po_send.at[k], po_recv.at[k], sibling)

    def finish_out(group):
        total = po_ref[group, 0, keep].astype(F32)
        for d in range(4):
            for core in range(2):
                if d > 0 or core == 1:
                    arrived(fr_ref.at[group, d, core], po_recv.at[(group * 4 + d) * 2 + core])
                    total = total + fr_ref[group, d, core].astype(F32)
        total = (total * jnp.tanh(gate[...])).astype(BF)
        for i in range(2):
            off = 2 * i - keep if group == 0 else 6 * i - 2 - keep
            rows = pl.ds(pl.multiple_of(zm(off) // 2 * 48, 16), 48)
            out[rows, :] = total[i * 48 : i * 48 + 48]

    combine(0)
    gather_near(0)
    combine(1)
    gather_near(1)
    gather_far(0)
    gather_far(1)
    for d in (1, 2, 3):
        arrived(ow_ref.at[ym(-d)], ow_recv.at[d - 1])
    project_out(0)
    gathered(0)
    gathered(1)
    project_out(1)
    finish_out(0)
    finish_out(1)

    for copy in sends:
        copy.wait_send()
    for kind in range(2):
        for d in (1, 2, 3):
            arrived(w_ref.at[kind, :, third[0], :], wx_send.at[kind, d - 1])
            arrived(a_ref.at[kind, y, t], f_send.at[kind, d - 1])
    arrived(a_ref.at[:, y, t], c_fsend.at[6])


def local(features, kv_weights, key_gain, queries, out_weight, attn_gate, group_images, tile_valid):
    anywhere = pl.BlockSpec(memory_space=pl.ANY)
    vmem = pl.BlockSpec(memory_space=pltpu.VMEM)
    smem = pl.BlockSpec(memory_space=pltpu.SMEM)
    dma = pltpu.SemaphoreType.DMA
    return pl.pallas_call(
        fused,
        out_shape=jax.ShapeDtypeStruct((192, 256), BF),
        in_specs=[anywhere, anywhere, vmem, anywhere, anywhere, vmem, anywhere, anywhere],
        out_specs=vmem,
        scratch_shapes=[
            pltpu.SMEM((2, 4), jnp.int32),
            pltpu.SMEM((4, 8), jnp.int32),
            pltpu.VMEM((2, NY, 2, 2, 32, 2048), BF),
            pltpu.VMEM((2, NZ, 256, 512), BF),
            pltpu.VMEM((2, 2, 4, 2, 256, HD), BF),
            pltpu.VMEM((2, 2, 2, 256, HD), BF),
            pltpu.VMEM((2, 2, 2, 2, 256, HD), BF),
            pltpu.VMEM((4, 3, 256, HD), BF),
            pltpu.VMEM((NX, 256, HD), BF),
            pltpu.VMEM((NX, 256, HD), BF),
            pltpu.VMEM((NX, 256, HD), BF),
            pltpu.VMEM((NX, 256, HD), BF),
            pltpu.VMEM((4, 256, HD), BF),
            pltpu.VMEM((1024, HD), BF),
            pltpu.VMEM((1024, HD), BF),
            pltpu.VMEM((192, 1024), BF),
            pltpu.VMEM((8, 192, 1024), BF),
            pltpu.VMEM((192, 1024), BF),
            pltpu.VMEM((192, 128), F32),
            pltpu.VMEM((2, 4, 48, 512), BF),
            pltpu.VMEM((4, 48, 128), F32),
            pltpu.VMEM((2, NZ, 48, 512), BF),
            pltpu.VMEM((NY, 1024, 256), BF),
            pltpu.VMEM((2, 4, 2, 96, 256), BF),
            pltpu.VMEM((2, 4, 2, 96, 256), BF),
            dma((9,)),
            dma((2, 3)), dma((2, 3)),
            dma((7,)), dma((7,)),
            dma((48,)), dma((48,)),
            dma((2, 3)), dma((2, 3)),
            dma((4, 6)), dma((4, 6)),
            dma((4, 3)), dma((4, 3)),
            dma((4,)), dma((4,)),
            dma((6,)), dma((6,)), dma((3,)), dma((3,)),
            dma((3,)), dma((3,)),
            dma((2, 8)), dma((2, 8)),
            dma((16,)), dma((16,)),
        ],
        compiler_params=pltpu.CompilerParams(
            collective_id=0, has_side_effects=True, vmem_limit_bytes=56 * 1024 * 1024
        ),
        name="fused",
    )(
        features, kv_weights, key_gain.reshape(1, HD), queries, out_weight,
        attn_gate.reshape(1, 1), group_images.T, tile_valid.T,
    )


def solution(mesh):
    placed = (
        P("group", ("img", "tensor"), None),
        P(None, "img", "tensor"),
        P(),
        P("group", "tensor"),
        P("tensor", "img"),
        P(),
        P(),
        P(),
    )
    return jax.shard_map(
        local, mesh=mesh, in_specs=placed, out_specs=P(("group", "tensor"), "img"), check_vma=False
    )
```

```python
import math

import jax
import jax.numpy as jnp
from jax import lax
from jax.experimental import pallas as pl
from jax.experimental.pallas import tpu as pltpu
from jax.sharding import PartitionSpec as P

HD = 128
MESH = pl.DeviceIdType.MESH
BF = jnp.bfloat16
F32 = jnp.float32
NX, NY, NZ = 4, 4, 8


def fused(
    feat, kvw, gain, queries, out_w, gate, images_hbm, counts_hbm, out,
    images, counts, a_ref, w_ref, p_ref, rs_relay, rs_recv, xs_ref, xk0_ref, xk1_ref, xv0_ref, xv1_ref, ps_ref, kb_ref, vb_ref,
    q_ref, pr_ref, o_ref, st_ref, zo_ref, zs_ref, at_ref, ow_ref, po_ref, fr_ref,
    loc_sem, f_send, f_recv, c_fsend, c_frecv, w_send, w_recv, wx_send, wx_recv,
    rs_send, rs_rsem, x_send, x_recv, pair_send, pair_recv, zo_send, zo_recv, zs_send, zs_recv,
    ow_send, ow_recv, g_send, g_recv, po_send, po_recv,
):
    x = lax.axis_index("group")
    img = lax.axis_index("img")
    t = lax.axis_index("tensor")
    z = img // NY
    y = img % NY
    other = 1 - t
    slot = z % 2

    def ym(d):
        return (y + d + NY) % NY

    def zm(d):
        return (z + d + NZ) % NZ

    def xm(d):
        return (x + d + NX) % NX

    def to_y(d):
        return {"img": z * NY + ym(d)}

    def to_z(d):
        return {"img": zm(d) * NY + y}

    def to_x(d):
        return {"group": xm(d)}

    sibling = {"tensor": other}
    partner = {"img": (z + 1 - 2 * slot) * NY + y}
    sends = []
    weight_sends = []

    def remote(src, dst, ssem, rsem, where):
        return pltpu.make_async_remote_copy(
            src_ref=src, dst_ref=dst, send_sem=ssem, recv_sem=rsem,
            device_id=where, device_id_type=MESH,
        )

    def send(src, dst, ssem, rsem, where):
        copy = remote(src, dst, ssem, rsem, where)
        copy.start()
        sends.append(copy)

    def drain(copies):
        for copy in copies:
            copy.wait_send()
        copies.clear()

    def arrived(ref, sem):
        pltpu.make_async_copy(ref, ref, sem).wait()

    locals_ = []

    def fetch(src, dst, sem):
        copy = pltpu.make_async_copy(src, dst, sem)
        copy.start()
        locals_.append(copy)

    third = (
        pl.ds(pl.multiple_of(128 + x * 32, 32), 32),
        pl.ds(pl.multiple_of(128 + x * 32, 16), 16),
        pl.ds(pl.multiple_of(128 + x * 32 + 16, 16), 16),
    )

    def columns(block, kind):
        return pl.ds(pl.multiple_of((block * NY + kind) * 256, 256), 256)

    def place(block):
        return pl.ds(pl.multiple_of(block * 256, 256), 256)

    barrier = pltpu.get_barrier_semaphore()
    partners = [sibling] + [to_y(d) for d in (1, 2, 3)] + [to_x(d) for d in (1, 2, 3)]
    partners += [to_z(d) for d in (1, 2, 4, 6, 7)]
    partners += [{**to_y(d), **sibling} for d in (1, 2, 3)]
    for where in partners:
        pl.semaphore_signal(barrier, inc=1, device_id=where, device_id_type=MESH)

    def fetch_own(block, carry):
        for half in range(2):
            own = feat.at[:, pl.ds(half * 32, 32), columns(block, y)]
            pltpu.make_async_copy(own, a_ref.at[half, y, t, :, :, place(block)], loc_sem.at[0]).start()
        return carry

    lax.fori_loop(0, NZ, fetch_own, 0)
    fetch(images_hbm, images, loc_sem.at[1])
    fetch(counts_hbm, counts, loc_sem.at[2])
    for kind in range(2):
        fetch(kvw.at[kind, pl.ds(0, 128), :], w_ref.at[kind, z, pl.ds(0, 128), :], loc_sem.at[3 + kind])
        fetch(kvw.at[kind, third[0], :], w_ref.at[kind, z, third[0], :], loc_sem.at[5 + kind])
    q_rows = pl.ds(pl.multiple_of(slot * 192, 64), 192)
    fetch(queries.at[q_rows, pl.ds(pl.multiple_of(y * 1024, 1024), 1024)], q_ref, loc_sem.at[7])
    mine = pl.ds(pl.multiple_of(y * 1024, 1024), 1024)
    fetch(out_w.at[mine, :], ow_ref.at[y], loc_sem.at[8])

    pl.semaphore_wait(barrier, len(partners))

    def w_parts(s, way):
        if s < 4:
            return (third[0], pl.ds(0, 64), pl.ds(64, 64))
        return (third[1 + way], pl.ds(64 * way, 64))

    def w_start(kind, s, way, part):
        rows = w_parts(s, way)[part]
        sign = 2 * way - 1
        origin = zm(sign * (s - 1))
        src = kvw.at[kind, rows, :] if s == 1 else w_ref.at[kind, origin, rows, :]
        k = ((kind * 2 + way) * 4 + s - 1) * 3 + part
        send(src, w_ref.at[kind, origin, rows, :], w_send.at[k], w_recv.at[k], to_z(-sign))

    def w_begin(kind):
        for part in range(3):
            for way in range(2):
                w_start(kind, 1, way, part)
        w_share(kind, (0,))

    def w_turn(kind, s):
        for part in range(3):
            for way in range(2):
                rows = w_parts(s, way)
                if part < len(rows):
                    k = ((kind * 2 + way) * 4 + s - 1) * 3 + part
                    arrived(w_ref.at[kind, zm((2 * way - 1) * s), rows[part], :], w_recv.at[k])
                if s < 3 or (s == 3 and (part == 0 or part == 1 + way)):
                    w_start(kind, s + 1, way, min(part, 1) if s == 3 else part)
            if part == 0:
                w_share(kind, (-s, s) if s < 4 else (4,))

    def w_share(kind, offsets):
        for off in offsets:
            dst = w_ref.at[kind, zm(off), third[0], :]
            src = kvw.at[kind, third[0], :] if off == 0 else dst
            for d in (2, 1, 3):
                remote(src, dst, wx_send.at[kind, d - 1], wx_recv.at[kind, d - 1], to_x(d)).start()

    def w_shared(kind):
        for d in (1, 2, 3):
            rows = pl.ds(pl.multiple_of(128 + xm(-d) * 32, 32), 32)
            arrived(w_ref.at[kind, :, rows, :], wx_recv.at[kind, d - 1])

    def start_half(half):
        def start(block, carry):
            for d in (2, 1, 3):
                remote(
                    feat.at[:, pl.ds(half * 32, 32), columns(block, ym(d))],
                    a_ref.at[half, y, t, :, :, place(block)],
                    f_send.at[half, d - 1], f_recv.at[half, d - 1], to_y(d),
                ).start()
            return carry

        lax.fori_loop(0, NZ, start, 0)

    def start_own(block, carry):
        for half in range(2):
            own = feat.at[:, pl.ds(half * 32, 32), columns(block, y)]
            remote(own, a_ref.at[half, y, t, :, :, place(block)], c_fsend.at[6], c_frecv.at[6], sibling).start()
        return carry

    def pass_half(half):
        for d in (1, 2, 3):
            block = a_ref.at[half, ym(-d), t]
            arrived(block, f_recv.at[half, d - 1])
            k = half * 3 + d - 1
            send(block, block, c_fsend.at[k], c_frecv.at[k], sibling)

    def project(kind, half, core):
        rows = (a_ref[half] if core is None else a_ref[half, :, core]).reshape(-1, 2048)
        part = jnp.dot(rows, w_ref[kind].reshape(2048, 512), preferred_element_type=F32).astype(BF)
        for src in range(4):
            for image in range(2):
                if core is None:
                    both = [part[src * 128 + c * 64 + image * 32 : src * 128 + c * 64 + image * 32 + 32] for c in range(2)]
                    rows = jnp.concatenate(both, axis=0)
                    where = pl.ds(src * 64, 64)
                else:
                    rows = part[src * 64 + image * 32 : src * 64 + image * 32 + 32]
                    where = pl.ds(pl.multiple_of(src * 64 + core * 32, 32), 32)
                for head in range(4):
                    p_ref[kind, half, head, image, where, :] = rows[:, head * 128 : head * 128 + 128]

    def siblings_rows(half):
        if half == 0:
            arrived(a_ref.at[:, y, other], c_frecv.at[6])
        for d in (1, 2, 3):
            arrived(a_ref.at[half, ym(-d), other], c_frecv.at[half * 3 + d - 1])

    def rs_start(kind, half):
        p, ss, rr = p_ref.at[kind, half], rs_send.at[kind * 2 + half], rs_rsem.at[kind * 2 + half]
        got, via = rs_recv.at[kind, half], rs_relay.at[kind, half]
        send(p.at[ym(2), 0], via.at[0], ss.at[0], rr.at[0], to_y(1))
        send(p.at[ym(2), 1], via.at[1], ss.at[1], rr.at[1], to_y(-1))
        send(p.at[ym(1), 1], got.at[0, 1], ss.at[2], rr.at[2], to_y(1))
        send(p.at[ym(-1), 0], got.at[1, 0], ss.at[3], rr.at[3], to_y(-1))

    def rs_middle(kind, half):
        p, ss, rr = p_ref.at[kind, half], rs_send.at[kind * 2 + half], rs_rsem.at[kind * 2 + half]
        got, via = rs_recv.at[kind, half], rs_relay.at[kind, half]
        for way, d in ((0, 1), (1, -1)):
            arrived(via.at[way], rr.at[way])
            p[ym(d), way] = (p[ym(d), way].astype(F32) + via[way].astype(F32)).astype(BF)
            send(p.at[ym(d), way], got.at[way, way], ss.at[4 + way], rr.at[4 + way], to_y(d))

    x_refs = (xk0_ref, xk1_ref, xv0_ref, xv1_ref)

    def rs_finish(kind, half):
        n = kind * 2 + half
        p, rr, got, xr_ref = p_ref.at[kind, half], rs_rsem.at[n], rs_recv.at[kind, half], x_refs[n]
        arrived(got.at[0, 1], rr.at[2])
        arrived(got.at[1, 0], rr.at[3])
        arrived(got.at[0, 0], rr.at[4])
        arrived(got.at[1, 1], rr.at[5])
        both = []
        for image in range(2):
            total = p[y, image].astype(F32) + got[0, image].astype(F32) + got[1, image].astype(F32)
            if kind == 0:
                mean = jnp.mean(total * total, axis=-1, keepdims=True)
                total = total * lax.rsqrt(mean + 1e-05) * gain[...]
            both.append(total.astype(BF))
        for d in (2, 1, 3, 0):
            group = xm(d)
            second = (images[0, group] == 2 * x + 1) | (images[1, group] == 2 * x + 1)
            block = jnp.where(second, both[1], both[0])
            if d == 0:
                xr_ref[x] = block
            else:
                xs_ref[n, d - 1] = block
                send(xs_ref.at[n, d - 1], xr_ref.at[x], x_send.at[n, d - 1], x_recv.at[n, d - 1], to_x(d))

    def pair(kind, half):
        n = kind * 2 + half
        xr_ref, both_ref = x_refs[n], (kb_ref, vb_ref)[kind]
        for d in range(1, NX):
            arrived(xr_ref.at[xm(-d)], x_recv.at[n, d - 1])
        ps_ref[n] = xr_ref[images[1 - slot, x] // 2]
        send(ps_ref.at[n], both_ref.at[pl.ds(512 + half * 256, 256)], pair_send.at[n], pair_recv.at[n], partner)
        both_ref[half * 256 : half * 256 + 256] = xr_ref[images[slot, x] // 2]

    def paired(kind):
        both_ref = (kb_ref, vb_ref)[kind]
        for half in range(2):
            arrived(both_ref.at[pl.ds(512 + half * 256, 256)], pair_recv.at[kind * 2 + half])

    w_begin(0)
    start_half(0)
    start_half(1)
    lax.fori_loop(0, NZ, start_own, 0)
    w_turn(0, 1)
    w_begin(1)
    w_turn(0, 2)
    w_turn(1, 1)
    pass_half(0)
    w_turn(0, 3)
    w_turn(1, 2)
    w_turn(0, 4)
    arrived(a_ref.at[:, y, t], loc_sem.at[0])
    for copy in locals_:
        copy.wait()
    w_shared(0)
    project(0, 0, t)
    siblings_rows(0)
    project(0, 0, other)
    rs_start(0, 0)
    pass_half(1)
    w_turn(1, 3)
    rs_middle(0, 0)
    w_turn(1, 4)
    project(0, 1, t)
    siblings_rows(1)
    project(0, 1, other)
    rs_start(0, 1)
    w_shared(1)
    project(1, 0, None)
    rs_start(1, 0)
    project(1, 1, None)
    rs_start(1, 1)
    rs_finish(0, 0)
    rs_middle(0, 1)
    rs_middle(1, 0)
    rs_middle(1, 1)
    rs_finish(0, 1)
    pair(0, 0)
    rs_finish(1, 0)
    rs_finish(1, 1)
    pair(0, 1)
    pair(1, 0)
    paired(0)

    image = images[slot, x]
    scale = 1.0 / math.sqrt(HD)
    lane = lax.broadcasted_iota(jnp.int32, (192, 128), 1)
    spot = lax.broadcasted_iota(jnp.int32, (1, 1024), 1)
    key_row = spot // 64 % 4 * 128 + spot // 32 % 2 * 64 + spot // 256 % 2 * 32 + spot % 32
    key_row = key_row + (spot // 512 + slot) % 2 * 512
    valid = jnp.broadcast_to(key_row, (192, 1024)) < counts[z // 2, image]

    def score_head(head, stats):
        q = q_ref[:, pl.ds(pl.multiple_of(head * 128, 128), 128)]
        s = lax.dot_general(q, kb_ref[...], (((1,), (1,)), ((), ())), preferred_element_type=F32) * scale
        s = jnp.where(valid, s, -1e30)
        peak = jnp.max(s, axis=-1, keepdims=True)
        e = jnp.exp(s - peak)
        total = jnp.sum(e, axis=-1, keepdims=True)
        pr_ref[head] = e.astype(BF)
        return jnp.where(lane == head, peak, jnp.where(lane == head + 8, total, stats))

    pair(1, 1)
    for d in (2, 1, 3):
        rows = pl.ds(pl.multiple_of(ym(d) * 1024, 1024), 1024)
        copy = remote(out_w.at[rows, :], ow_ref.at[y], ow_send.at[d - 1], ow_recv.at[d - 1], to_y(d))
        copy.start()
        weight_sends.append(copy)
    st_ref[...] = lax.fori_loop(0, 8, score_head, jnp.zeros((192, 128), F32))

    def share_of(d):
        return pl.ds(pl.multiple_of(zm(d) // 2 * 48, 16), 48)

    for k, d in enumerate((2, 4, 6)):
        send(st_ref.at[share_of(d), :], zs_ref.at[k + 1], zs_send.at[k], zs_recv.at[k], to_z(d))
    zs_ref[0] = st_ref[share_of(0), :]

    paired(1)

    def weigh_head(head, carry):
        o = jnp.dot(pr_ref[head], vb_ref[...], preferred_element_type=F32)
        o_ref[:, pl.ds(pl.multiple_of(head * 128, 128), 128)] = o.astype(BF)
        return carry

    early = list(sends)
    sends.clear()

    for half in range(2):
        lax.fori_loop(half * 4, half * 4 + 4, weigh_head, 0)
        for k, d in enumerate((2, 4, 6)):
            n = half * 3 + k
            part = o_ref.at[share_of(d), pl.ds(half * 512, 512)]
            send(part, zo_ref.at[half, k + 1], zo_send.at[n], zo_recv.at[n], to_z(d))
        zo_ref[half, 0] = o_ref[share_of(0), half * 512 : half * 512 + 512]
    drain(early)
    for kind in range(2):
        for d in (1, 2, 3):
            arrived(w_ref.at[kind, :, third[0], :], wx_send.at[kind, d - 1])
            arrived(a_ref.at[kind, y, t], f_send.at[kind, d - 1])
    arrived(a_ref.at[:, y, t], c_fsend.at[6])
    for k in range(3):
        arrived(zs_ref.at[k + 1], zs_recv.at[k])
    stats = [zs_ref[k] for k in range(4)]
    peak = jnp.maximum(jnp.maximum(stats[0], stats[1]), jnp.maximum(stats[2], stats[3]))
    shares = [jnp.exp(s - peak) for s in stats]
    total = jnp.zeros((48, 128), F32)
    for k in range(4):
        total = total + shares[k] * pltpu.roll(stats[k], 120, 1)
    shares = [share / total for share in shares]

    def combine(half):
        for k in range(3):
            arrived(zo_ref.at[half, k + 1], zo_recv.at[half * 3 + k])
        for head in range(4):
            cols = pl.ds(head * 128, 128)
            h = half * 4 + head
            sums = jnp.zeros((48, 128), F32)
            for k in range(4):
                sums = sums + zo_ref[half, k, :, cols].astype(F32) * shares[k][:, h : h + 1]
            done = sums.astype(BF)
            at_ref[half, z, :, cols] = done

    def gather_near(half):
        block = at_ref.at[half, z]
        for d in (2, 6, 1, 7):
            send(block, block, g_send.at[half, d], g_recv.at[half, d], to_z(d))

    def gather_far(half):
        for d in (2, 6):
            arrived(at_ref.at[half, zm(-d)], g_recv.at[half, d])
        across = 2 if half == 0 else 6
        block = at_ref.at[half, zm(-across)]
        send(block, block, g_send.at[half, 4], g_recv.at[half, 4], to_z(across))
        for d in (1, 7):
            block = at_ref.at[half, zm(-2 if d == 1 else 2)]
            k = 3 if d == 1 else 5
            send(block, block, g_send.at[half, k], g_recv.at[half, k], to_z(d))

    def gathered(half):
        for k in (4, 3, 5):
            arrived(at_ref.at[half, zm(-k)], g_recv.at[half, k])

    keep = (z + t) % 2

    def project_out(group):
        offsets = (0, 2, -1, 1) if group == 0 else (-2, 4, -3, 3)
        rows = [
            jnp.concatenate([at_ref[half, zm(off)] for off in offsets], axis=0) for half in range(2)
        ]
        for d in (2, 1, 3, 0):
            part = jnp.dot(rows[0], ow_ref[ym(d), 0:512], preferred_element_type=F32)
            part = part + jnp.dot(rows[1], ow_ref[ym(d), 512:1024], preferred_element_type=F32)
            part = part.astype(BF)
            po_ref[group, d, 0] = part[0:96]
            po_ref[group, d, 1] = part[96:192]
            for core in range(2):
                block = po_ref.at[group, d, (keep + core) % 2]
                k = (group * 4 + d) * 2 + core
                if d > 0:
                    where = to_y(d) if core == 0 else {**to_y(d), **sibling}
                    send(block, fr_ref.at[group, d, core], po_send.at[k], po_recv.at[k], where)
                elif core == 1:
                    send(block, fr_ref.at[group, d, core], po_send.at[k], po_recv.at[k], sibling)

    def finish_out(group):
        total = po_ref[group, 0, keep].astype(F32)
        for d in range(4):
            for core in range(2):
                if d > 0 or core == 1:
                    arrived(fr_ref.at[group, d, core], po_recv.at[(group * 4 + d) * 2 + core])
                    total = total + fr_ref[group, d, core].astype(F32)
        total = (total * jnp.tanh(gate[...])).astype(BF)
        for i in range(2):
            off = 2 * i - keep if group == 0 else 6 * i - 2 - keep
            rows = pl.ds(pl.multiple_of(zm(off) // 2 * 48, 16), 48)
            out[rows, :] = total[i * 48 : i * 48 + 48]

    combine(0)
    gather_near(0)
    combine(1)
    gather_near(1)
    gather_far(0)
    gather_far(1)
    for d in (1, 2, 3):
        arrived(ow_ref.at[ym(-d)], ow_recv.at[d - 1])
    for half in range(2):
        for d in (1, 7):
            arrived(at_ref.at[half, zm(-d)], g_recv.at[half, d])
    project_out(0)
    early = list(sends)
    sends.clear()
    gathered(0)
    gathered(1)
    project_out(1)
    drain(early)
    drain(weight_sends)
    finish_out(0)
    finish_out(1)

    drain(sends)


def local(features, kv_weights, key_gain, queries, out_weight, attn_gate, group_images, tile_valid):
    anywhere = pl.BlockSpec(memory_space=pl.ANY)
    vmem = pl.BlockSpec(memory_space=pltpu.VMEM)
    smem = pl.BlockSpec(memory_space=pltpu.SMEM)
    dma = pltpu.SemaphoreType.DMA
    return pl.pallas_call(
        fused,
        out_shape=jax.ShapeDtypeStruct((192, 256), BF),
        in_specs=[anywhere, anywhere, vmem, anywhere, anywhere, vmem, anywhere, anywhere],
        out_specs=vmem,
        scratch_shapes=[
            pltpu.SMEM((2, 4), jnp.int32),
            pltpu.SMEM((4, 8), jnp.int32),
            pltpu.VMEM((2, NY, 2, 2, 32, 2048), BF),
            pltpu.VMEM((2, NZ, 256, 512), BF),
            pltpu.VMEM((2, 2, 4, 2, 256, HD), BF),
            pltpu.VMEM((2, 2, 2, 256, HD), BF),
            pltpu.VMEM((2, 2, 2, 2, 256, HD), BF),
            pltpu.VMEM((4, 3, 256, HD), BF),
            pltpu.VMEM((NX, 256, HD), BF),
            pltpu.VMEM((NX, 256, HD), BF),
            pltpu.VMEM((NX, 256, HD), BF),
            pltpu.VMEM((NX, 256, HD), BF),
            pltpu.VMEM((4, 256, HD), BF),
            pltpu.VMEM((1024, HD), BF),
            pltpu.VMEM((1024, HD), BF),
            pltpu.VMEM((192, 1024), BF),
            pltpu.VMEM((8, 192, 1024), BF),
            pltpu.VMEM((192, 1024), BF),
            pltpu.VMEM((192, 128), F32),
            pltpu.VMEM((2, 4, 48, 512), BF),
            pltpu.VMEM((4, 48, 128), F32),
            pltpu.VMEM((2, NZ, 48, 512), BF),
            pltpu.VMEM((NY, 1024, 256), BF),
            pltpu.VMEM((2, 4, 2, 96, 256), BF),
            pltpu.VMEM((2, 4, 2, 96, 256), BF),
            dma((9,)),
            dma((2, 3)), dma((2, 3)),
            dma((7,)), dma((7,)),
            dma((48,)), dma((48,)),
            dma((2, 3)), dma((2, 3)),
            dma((4, 6)), dma((4, 6)),
            dma((4, 3)), dma((4, 3)),
            dma((4,)), dma((4,)),
            dma((6,)), dma((6,)), dma((3,)), dma((3,)),
            dma((3,)), dma((3,)),
            dma((2, 8)), dma((2, 8)),
            dma((16,)), dma((16,)),
        ],
        compiler_params=pltpu.CompilerParams(
            collective_id=0, has_side_effects=True, vmem_limit_bytes=56 * 1024 * 1024
        ),
        name="fused",
    )(
        features, kv_weights, key_gain.reshape(1, HD), queries, out_weight,
        attn_gate.reshape(1, 1), group_images.T, tile_valid.T,
    )


def solution(mesh):
    placed = (
        P("group", ("img", "tensor"), None),
        P(None, "img", "tensor"),
        P(),
        P("group", "tensor"),
        P("tensor", "img"),
        P(),
        P(),
        P(),
    )
    return jax.shard_map(
        local, mesh=mesh, in_specs=placed, out_specs=P(("group", "tensor"), "img"), check_vma=False
    )
```

```python
import math

import jax
import jax.numpy as jnp
from jax import lax
from jax.experimental import pallas as pl
from jax.experimental.pallas import tpu as pltpu
from jax.sharding import PartitionSpec as P

HD = 128
MESH = pl.DeviceIdType.MESH
BF = jnp.bfloat16
F32 = jnp.float32
NX, NY, NZ = 4, 4, 8


def fused(
    feat, kvw, gain, queries, out_w, gate, images_hbm, counts_hbm, out,
    images, counts, a_ref, w_ref, p_ref, rs_relay, rs_recv, xs_ref, xk0_ref, xk1_ref, xv0_ref, xv1_ref, ps_ref, kb_ref, vb_ref,
    q_ref, pr_ref, o_ref, st_ref, zo_ref, zs_ref, at_ref, ow_ref, po_ref, fr_ref,
    loc_sem, f_send, f_recv, c_fsend, c_frecv, w_send, w_recv, wx_send, wx_recv,
    rs_send, rs_rsem, x_send, x_recv, pair_send, pair_recv, zo_send, zo_recv, zs_send, zs_recv,
    ow_send, ow_recv, g_send, g_recv, po_send, po_recv,
):
    x = lax.axis_index("group")
    img = lax.axis_index("img")
    t = lax.axis_index("tensor")
    z = img // NY
    y = img % NY
    other = 1 - t
    slot = z % 2

    def ym(d):
        return (y + d + NY) % NY

    def zm(d):
        return (z + d + NZ) % NZ

    def xm(d):
        return (x + d + NX) % NX

    def to_y(d):
        return {"img": z * NY + ym(d)}

    def to_z(d):
        return {"img": zm(d) * NY + y}

    def to_x(d):
        return {"group": xm(d)}

    sibling = {"tensor": other}
    partner = {"img": (z + 1 - 2 * slot) * NY + y}
    sends = []
    weight_sends = []

    def remote(src, dst, ssem, rsem, where):
        return pltpu.make_async_remote_copy(
            src_ref=src, dst_ref=dst, send_sem=ssem, recv_sem=rsem,
            device_id=where, device_id_type=MESH,
        )

    def send(src, dst, ssem, rsem, where):
        copy = remote(src, dst, ssem, rsem, where)
        copy.start()
        sends.append(copy)

    def drain(copies):
        for copy in copies:
            copy.wait_send()
        copies.clear()

    def arrived(ref, sem):
        pltpu.make_async_copy(ref, ref, sem).wait()

    locals_ = []

    def fetch(src, dst, sem):
        copy = pltpu.make_async_copy(src, dst, sem)
        copy.start()
        locals_.append(copy)

    third = (
        pl.ds(pl.multiple_of(128 + x * 32, 32), 32),
        pl.ds(pl.multiple_of(128 + x * 32, 16), 16),
        pl.ds(pl.multiple_of(128 + x * 32 + 16, 16), 16),
    )

    def columns(block, kind):
        return pl.ds(pl.multiple_of((block * NY + kind) * 256, 256), 256)

    def place(block):
        return pl.ds(pl.multiple_of(block * 256, 256), 256)

    barrier = pltpu.get_barrier_semaphore()
    partners = [sibling] + [to_y(d) for d in (1, 2, 3)] + [to_x(d) for d in (1, 2, 3)]
    partners += [to_z(d) for d in (1, 2, 4, 6, 7)]
    partners += [{**to_y(d), **sibling} for d in (1, 2, 3)]
    for where in partners:
        pl.semaphore_signal(barrier, inc=1, device_id=where, device_id_type=MESH)

    def fetch_own(block, carry):
        for half in range(2):
            own = feat.at[:, pl.ds(half * 32, 32), columns(block, y)]
            pltpu.make_async_copy(own, a_ref.at[half, y, t, :, :, place(block)], loc_sem.at[0]).start()
        return carry

    lax.fori_loop(0, NZ, fetch_own, 0)
    fetch(images_hbm, images, loc_sem.at[1])
    fetch(counts_hbm, counts, loc_sem.at[2])
    for kind in range(2):
        fetch(kvw.at[kind, pl.ds(0, 128), :], w_ref.at[kind, z, pl.ds(0, 128), :], loc_sem.at[3 + kind])
        fetch(kvw.at[kind, third[0], :], w_ref.at[kind, z, third[0], :], loc_sem.at[5 + kind])
    q_rows = pl.ds(pl.multiple_of(slot * 192, 64), 192)
    fetch(queries.at[q_rows, pl.ds(pl.multiple_of(y * 1024, 1024), 1024)], q_ref, loc_sem.at[7])
    mine = pl.ds(pl.multiple_of(y * 1024, 1024), 1024)
    fetch(out_w.at[mine, :], ow_ref.at[y], loc_sem.at[8])

    pl.semaphore_wait(barrier, len(partners))

    def w_parts(s, way):
        if s < 4:
            return (third[0], pl.ds(0, 64), pl.ds(64, 64))
        return (third[1 + way], pl.ds(64 * way, 64))

    def w_start(kind, s, way, part):
        rows = w_parts(s, way)[part]
        sign = 2 * way - 1
        origin = zm(sign * (s - 1))
        src = kvw.at[kind, rows, :] if s == 1 else w_ref.at[kind, origin, rows, :]
        k = ((kind * 2 + way) * 4 + s - 1) * 3 + part
        send(src, w_ref.at[kind, origin, rows, :], w_send.at[k], w_recv.at[k], to_z(-sign))

    def w_begin(kind):
        for part in range(3):
            for way in range(2):
                w_start(kind, 1, way, part)
        w_share(kind, (0,))

    def w_turn(kind, s):
        for part in range(3):
            for way in range(2):
                rows = w_parts(s, way)
                if part < len(rows):
                    k = ((kind * 2 + way) * 4 + s - 1) * 3 + part
                    arrived(w_ref.at[kind, zm((2 * way - 1) * s), rows[part], :], w_recv.at[k])
                if s < 3 or (s == 3 and (part == 0 or part == 1 + way)):
                    w_start(kind, s + 1, way, min(part, 1) if s == 3 else part)
            if part == 0:
                w_share(kind, (-s, s) if s < 4 else (4,))

    def w_share(kind, offsets):
        for off in offsets:
            dst = w_ref.at[kind, zm(off), third[0], :]
            src = kvw.at[kind, third[0], :] if off == 0 else dst
            for d in (2, 1, 3):
                remote(src, dst, wx_send.at[kind, d - 1], wx_recv.at[kind, d - 1], to_x(d)).start()

    def w_shared(kind):
        for d in (1, 2, 3):
            rows = pl.ds(pl.multiple_of(128 + xm(-d) * 32, 32), 32)
            arrived(w_ref.at[kind, :, rows, :], wx_recv.at[kind, d - 1])

    def start_half(half):
        def start(block, carry):
            for d in (2, 1, 3):
                remote(
                    feat.at[:, pl.ds(half * 32, 32), columns(block, ym(d))],
                    a_ref.at[half, y, t, :, :, place(block)],
                    f_send.at[half, d - 1], f_recv.at[half, d - 1], to_y(d),
                ).start()
            return carry

        lax.fori_loop(0, NZ, start, 0)

    def start_own(block, carry):
        for half in range(2):
            own = feat.at[:, pl.ds(half * 32, 32), columns(block, y)]
            remote(own, a_ref.at[half, y, t, :, :, place(block)], c_fsend.at[6], c_frecv.at[6], sibling).start()
        return carry

    def pass_half(half):
        for d in (1, 2, 3):
            block = a_ref.at[half, ym(-d), t]
            arrived(block, f_recv.at[half, d - 1])
            k = half * 3 + d - 1
            send(block, block, c_fsend.at[k], c_frecv.at[k], sibling)

    def project(kind, half, core):
        rows = (a_ref[half] if core is None else a_ref[half, :, core]).reshape(-1, 2048)
        part = jnp.dot(rows, w_ref[kind].reshape(2048, 512), preferred_element_type=F32).astype(BF)
        for src in range(4):
            for image in range(2):
                if core is None:
                    both = [part[src * 128 + c * 64 + image * 32 : src * 128 + c * 64 + image * 32 + 32] for c in range(2)]
                    rows = jnp.concatenate(both, axis=0)
                    where = pl.ds(src * 64, 64)
                else:
                    rows = part[src * 64 + image * 32 : src * 64 + image * 32 + 32]
                    where = pl.ds(pl.multiple_of(src * 64 + core * 32, 32), 32)
                for head in range(4):
                    p_ref[kind, half, head, image, where, :] = rows[:, head * 128 : head * 128 + 128]

    def siblings_rows(half):
        if half == 0:
            arrived(a_ref.at[:, y, other], c_frecv.at[6])
        for d in (1, 2, 3):
            arrived(a_ref.at[half, ym(-d), other], c_frecv.at[half * 3 + d - 1])

    def rs_start(kind, half):
        p, ss, rr = p_ref.at[kind, half], rs_send.at[kind * 2 + half], rs_rsem.at[kind * 2 + half]
        got, via = rs_recv.at[kind, half], rs_relay.at[kind, half]
        send(p.at[ym(2), 0], via.at[0], ss.at[0], rr.at[0], to_y(1))
        send(p.at[ym(2), 1], via.at[1], ss.at[1], rr.at[1], to_y(-1))
        send(p.at[ym(1), 1], got.at[0, 1], ss.at[2], rr.at[2], to_y(1))
        send(p.at[ym(-1), 0], got.at[1, 0], ss.at[3], rr.at[3], to_y(-1))

    def rs_middle(kind, half):
        p, ss, rr = p_ref.at[kind, half], rs_send.at[kind * 2 + half], rs_rsem.at[kind * 2 + half]
        got, via = rs_recv.at[kind, half], rs_relay.at[kind, half]
        for way, d in ((0, 1), (1, -1)):
            arrived(via.at[way], rr.at[way])
            p[ym(d), way] = (p[ym(d), way].astype(F32) + via[way].astype(F32)).astype(BF)
            send(p.at[ym(d), way], got.at[way, way], ss.at[4 + way], rr.at[4 + way], to_y(d))

    x_refs = (xk0_ref, xk1_ref, xv0_ref, xv1_ref)

    def rs_finish(kind, half):
        n = kind * 2 + half
        p, rr, got, xr_ref = p_ref.at[kind, half], rs_rsem.at[n], rs_recv.at[kind, half], x_refs[n]
        arrived(got.at[0, 1], rr.at[2])
        arrived(got.at[1, 0], rr.at[3])
        arrived(got.at[0, 0], rr.at[4])
        arrived(got.at[1, 1], rr.at[5])
        both = []
        for image in range(2):
            total = p[y, image].astype(F32) + got[0, image].astype(F32) + got[1, image].astype(F32)
            if kind == 0:
                mean = jnp.mean(total * total, axis=-1, keepdims=True)
                total = total * lax.rsqrt(mean + 1e-05) * gain[...]
            both.append(total.astype(BF))
        for d in (2, 1, 3, 0):
            group = xm(d)
            second = (images[0, group] == 2 * x + 1) | (images[1, group] == 2 * x + 1)
            block = jnp.where(second, both[1], both[0])
            if d == 0:
                xr_ref[x] = block
            else:
                xs_ref[n, d - 1] = block
                send(xs_ref.at[n, d - 1], xr_ref.at[x], x_send.at[n, d - 1], x_recv.at[n, d - 1], to_x(d))

    def pair(kind, half):
        n = kind * 2 + half
        xr_ref, both_ref = x_refs[n], (kb_ref, vb_ref)[kind]
        for d in range(1, NX):
            arrived(xr_ref.at[xm(-d)], x_recv.at[n, d - 1])
        ps_ref[n] = xr_ref[images[1 - slot, x] // 2]
        send(ps_ref.at[n], both_ref.at[pl.ds(512 + half * 256, 256)], pair_send.at[n], pair_recv.at[n], partner)
        both_ref[half * 256 : half * 256 + 256] = xr_ref[images[slot, x] // 2]

    def paired(kind):
        both_ref = (kb_ref, vb_ref)[kind]
        for half in range(2):
            arrived(both_ref.at[pl.ds(512 + half * 256, 256)], pair_recv.at[kind * 2 + half])

    w_begin(0)
    start_half(0)
    start_half(1)
    lax.fori_loop(0, NZ, start_own, 0)
    w_turn(0, 1)
    w_begin(1)
    w_turn(0, 2)
    w_turn(1, 1)
    pass_half(0)
    w_turn(0, 3)
    w_turn(1, 2)
    w_turn(0, 4)
    arrived(a_ref.at[:, y, t], loc_sem.at[0])
    for copy in locals_:
        copy.wait()
    w_shared(0)
    project(0, 0, t)
    siblings_rows(0)
    project(0, 0, other)
    rs_start(0, 0)
    pass_half(1)
    w_turn(1, 3)
    rs_middle(0, 0)
    w_turn(1, 4)
    project(0, 1, t)
    siblings_rows(1)
    project(0, 1, other)
    rs_start(0, 1)
    w_shared(1)
    project(1, 0, None)
    rs_start(1, 0)
    project(1, 1, None)
    rs_start(1, 1)
    rs_finish(0, 0)
    rs_middle(0, 1)
    rs_middle(1, 0)
    rs_middle(1, 1)
    rs_finish(0, 1)
    pair(0, 0)
    rs_finish(1, 0)
    rs_finish(1, 1)
    pair(0, 1)
    pair(1, 0)
    paired(0)

    image = images[slot, x]
    scale = 1.0 / math.sqrt(HD)
    lane = lax.broadcasted_iota(jnp.int32, (192, 128), 1)
    spot = lax.broadcasted_iota(jnp.int32, (1, 1024), 1)
    key_row = spot // 64 % 4 * 128 + spot // 32 % 2 * 64 + spot // 256 % 2 * 32 + spot % 32
    key_row = key_row + (spot // 512 + slot) % 2 * 512
    valid = jnp.broadcast_to(key_row, (192, 1024)) < counts[z // 2, image]

    def score_head(head, stats):
        q = q_ref[:, pl.ds(pl.multiple_of(head * 128, 128), 128)]
        s = lax.dot_general(q, kb_ref[...], (((1,), (1,)), ((), ())), preferred_element_type=F32) * scale
        s = jnp.where(valid, s, -1e30)
        peak = jnp.max(s, axis=-1, keepdims=True)
        e = jnp.exp(s - peak)
        total = jnp.sum(e, axis=-1, keepdims=True)
        pr_ref[head] = e.astype(BF)
        return jnp.where(lane == head, peak, jnp.where(lane == head + 8, total, stats))

    stats = lax.fori_loop(0, 2, score_head, jnp.zeros((192, 128), F32))
    pair(1, 1)
    for d in (2, 1, 3):
        rows = pl.ds(pl.multiple_of(ym(d) * 1024, 1024), 1024)
        copy = remote(out_w.at[rows, :], ow_ref.at[y], ow_send.at[d - 1], ow_recv.at[d - 1], to_y(d))
        copy.start()
        weight_sends.append(copy)
    st_ref[...] = lax.fori_loop(2, 8, score_head, stats)

    def share_of(d):
        return pl.ds(pl.multiple_of(zm(d) // 2 * 48, 16), 48)

    for k, d in enumerate((2, 4, 6)):
        send(st_ref.at[share_of(d), :], zs_ref.at[k + 1], zs_send.at[k], zs_recv.at[k], to_z(d))
    zs_ref[0] = st_ref[share_of(0), :]

    paired(1)

    def weigh_head(head, carry):
        o = jnp.dot(pr_ref[head], vb_ref[...], preferred_element_type=F32)
        o_ref[:, pl.ds(pl.multiple_of(head * 128, 128), 128)] = o.astype(BF)
        return carry

    early = list(sends)
    sends.clear()

    for half in range(2):
        lax.fori_loop(half * 4, half * 4 + 4, weigh_head, 0)
        for k, d in enumerate((2, 4, 6)):
            n = half * 3 + k
            part = o_ref.at[share_of(d), pl.ds(half * 512, 512)]
            send(part, zo_ref.at[half, k + 1], zo_send.at[n], zo_recv.at[n], to_z(d))
        zo_ref[half, 0] = o_ref[share_of(0), half * 512 : half * 512 + 512]
    drain(early)
    for kind in range(2):
        for d in (1, 2, 3):
            arrived(w_ref.at[kind, :, third[0], :], wx_send.at[kind, d - 1])
            arrived(a_ref.at[kind, y, t], f_send.at[kind, d - 1])
    arrived(a_ref.at[:, y, t], c_fsend.at[6])
    for k in range(3):
        arrived(zs_ref.at[k + 1], zs_recv.at[k])
    stats = [zs_ref[k] for k in range(4)]
    peak = jnp.maximum(jnp.maximum(stats[0], stats[1]), jnp.maximum(stats[2], stats[3]))
    shares = [jnp.exp(s - peak) for s in stats]
    total = jnp.zeros((48, 128), F32)
    for k in range(4):
        total = total + shares[k] * pltpu.roll(stats[k], 120, 1)
    shares = [share / total for share in shares]

    def combine(half):
        for k in range(3):
            arrived(zo_ref.at[half, k + 1], zo_recv.at[half * 3 + k])
        for head in range(4):
            cols = pl.ds(head * 128, 128)
            h = half * 4 + head
            sums = jnp.zeros((48, 128), F32)
            for k in range(4):
                sums = sums + zo_ref[half, k, :, cols].astype(F32) * shares[k][:, h : h + 1]
            done = sums.astype(BF)
            at_ref[half, z, :, cols] = done

    def gather_near(half):
        block = at_ref.at[half, z]
        for d in (2, 6, 1, 7):
            send(block, block, g_send.at[half, d], g_recv.at[half, d], to_z(d))

    def gather_far(half):
        for d in (2, 6):
            arrived(at_ref.at[half, zm(-d)], g_recv.at[half, d])
        across = 2 if half == 0 else 6
        block = at_ref.at[half, zm(-across)]
        send(block, block, g_send.at[half, 4], g_recv.at[half, 4], to_z(across))
        for d in (1, 7):
            block = at_ref.at[half, zm(-2 if d == 1 else 2)]
            k = 3 if d == 1 else 5
            send(block, block, g_send.at[half, k], g_recv.at[half, k], to_z(d))

    def gathered(half):
        for k in (4, 3, 5):
            arrived(at_ref.at[half, zm(-k)], g_recv.at[half, k])

    keep = (z + t) % 2

    def project_out(group):
        offsets = (0, 2, -1, 1) if group == 0 else (-2, 4, -3, 3)
        rows = [
            jnp.concatenate([at_ref[half, zm(off)] for off in offsets], axis=0) for half in range(2)
        ]
        for d in (2, 1, 3, 0):
            part = jnp.dot(rows[0], ow_ref[ym(d), 0:512], preferred_element_type=F32)
            part = part + jnp.dot(rows[1], ow_ref[ym(d), 512:1024], preferred_element_type=F32)
            part = part.astype(BF)
            po_ref[group, d, 0] = part[0:96]
            po_ref[group, d, 1] = part[96:192]
            for core in range(2):
                block = po_ref.at[group, d, (keep + core) % 2]
                k = (group * 4 + d) * 2 + core
                if d > 0:
                    where = to_y(d) if core == 0 else {**to_y(d), **sibling}
                    send(block, fr_ref.at[group, d, core], po_send.at[k], po_recv.at[k], where)
                elif core == 1:
                    send(block, fr_ref.at[group, d, core], po_send.at[k], po_recv.at[k], sibling)

    def finish_out(group):
        total = po_ref[group, 0, keep].astype(F32)
        for d in range(4):
            for core in range(2):
                if d > 0 or core == 1:
                    arrived(fr_ref.at[group, d, core], po_recv.at[(group * 4 + d) * 2 + core])
                    total = total + fr_ref[group, d, core].astype(F32)
        total = (total * jnp.tanh(gate[...])).astype(BF)
        for i in range(2):
            off = 2 * i - keep if group == 0 else 6 * i - 2 - keep
            rows = pl.ds(pl.multiple_of(zm(off) // 2 * 48, 16), 48)
            out[rows, :] = total[i * 48 : i * 48 + 48]

    combine(0)
    gather_near(0)
    combine(1)
    gather_near(1)
    gather_far(0)
    gather_far(1)
    for d in (1, 2, 3):
        arrived(ow_ref.at[ym(-d)], ow_recv.at[d - 1])
    for half in range(2):
        for d in (1, 7):
            arrived(at_ref.at[half, zm(-d)], g_recv.at[half, d])
    project_out(0)
    early = list(sends)
    sends.clear()
    gathered(0)
    gathered(1)
    project_out(1)
    drain(early)
    drain(weight_sends)
    finish_out(0)
    finish_out(1)

    drain(sends)


def local(features, kv_weights, key_gain, queries, out_weight, attn_gate, group_images, tile_valid):
    anywhere = pl.BlockSpec(memory_space=pl.ANY)
    vmem = pl.BlockSpec(memory_space=pltpu.VMEM)
    smem = pl.BlockSpec(memory_space=pltpu.SMEM)
    dma = pltpu.SemaphoreType.DMA
    return pl.pallas_call(
        fused,
        out_shape=jax.ShapeDtypeStruct((192, 256), BF),
        in_specs=[anywhere, anywhere, vmem, anywhere, anywhere, vmem, anywhere, anywhere],
        out_specs=vmem,
        scratch_shapes=[
            pltpu.SMEM((2, 4), jnp.int32),
            pltpu.SMEM((4, 8), jnp.int32),
            pltpu.VMEM((2, NY, 2, 2, 32, 2048), BF),
            pltpu.VMEM((2, NZ, 256, 512), BF),
            pltpu.VMEM((2, 2, 4, 2, 256, HD), BF),
            pltpu.VMEM((2, 2, 2, 256, HD), BF),
            pltpu.VMEM((2, 2, 2, 2, 256, HD), BF),
            pltpu.VMEM((4, 3, 256, HD), BF),
            pltpu.VMEM((NX, 256, HD), BF),
            pltpu.VMEM((NX, 256, HD), BF),
            pltpu.VMEM((NX, 256, HD), BF),
            pltpu.VMEM((NX, 256, HD), BF),
            pltpu.VMEM((4, 256, HD), BF),
            pltpu.VMEM((1024, HD), BF),
            pltpu.VMEM((1024, HD), BF),
            pltpu.VMEM((192, 1024), BF),
            pltpu.VMEM((8, 192, 1024), BF),
            pltpu.VMEM((192, 1024), BF),
            pltpu.VMEM((192, 128), F32),
            pltpu.VMEM((2, 4, 48, 512), BF),
            pltpu.VMEM((4, 48, 128), F32),
            pltpu.VMEM((2, NZ, 48, 512), BF),
            pltpu.VMEM((NY, 1024, 256), BF),
            pltpu.VMEM((2, 4, 2, 96, 256), BF),
            pltpu.VMEM((2, 4, 2, 96, 256), BF),
            dma((9,)),
            dma((2, 3)), dma((2, 3)),
            dma((7,)), dma((7,)),
            dma((48,)), dma((48,)),
            dma((2, 3)), dma((2, 3)),
            dma((4, 6)), dma((4, 6)),
            dma((4, 3)), dma((4, 3)),
            dma((4,)), dma((4,)),
            dma((6,)), dma((6,)), dma((3,)), dma((3,)),
            dma((3,)), dma((3,)),
            dma((2, 8)), dma((2, 8)),
            dma((16,)), dma((16,)),
        ],
        compiler_params=pltpu.CompilerParams(
            collective_id=0, has_side_effects=True, vmem_limit_bytes=56 * 1024 * 1024
        ),
        name="fused",
    )(
        features, kv_weights, key_gain.reshape(1, HD), queries, out_weight,
        attn_gate.reshape(1, 1), group_images.T, tile_valid.T,
    )


def solution(mesh):
    placed = (
        P("group", ("img", "tensor"), None),
        P(None, "img", "tensor"),
        P(),
        P("group", "tensor"),
        P("tensor", "img"),
        P(),
        P(),
        P(),
    )
    return jax.shard_map(
        local, mesh=mesh, in_specs=placed, out_specs=P(("group", "tensor"), "img"), check_vma=False
    )
```
